256 devices in a mesh: blk: 64 (over z, x, core), head: 4 (over y).
Axes of the slice: x: 4, y: 4, z: 8, core: 2. Of those that a mesh axis runs over, the one named last changes fastest.
Arguments:
- queries: bfloat16 [128, 128, 128], P('blk', 'head'), may hold values from -120 to 120
- cache_keys: bfloat16 [131072, 8, 128], P('blk', 'head'), may hold values from -5 to 5
- cache_values: bfloat16 [131072, 8, 128], P('blk', 'head'), may hold values from -6 to 6
- stretch_keys: bfloat16 [128, 8, 128], P('blk', 'head'), may hold values from -12 to 12
- stretch_values: bfloat16 [128, 8, 128], P('blk', 'head'), may hold values from -6 to 6
- valid_lens: int32 [64], P('blk'), may hold values from 1024 to 2048
- offsets: int32 [4], replicated, may hold values from 65536 to 131072
- seq_lengths: int32 [4], replicated, may hold values from 1 to 64, 128 in all
- out_weight: bfloat16 [16384, 16384], P('head', 'blk'), may hold values from -0.046875 to 0.046875
Outputs:
- mixed: bfloat16 [128, 16384], P('head', 'blk')
The draws below stay inside these ranges and needn't reach their ends.
Inputs may be any that keep to these rules, and one draw needn't show every extreme that they name: `seq_lengths`: the lengths sum to 128; the longest completion has exactly 64 tokens.
All inputs are finite; a program needn't handle non-finite values.
Results may differ from the reference program's by a relative error of at most 0.0048.
Values may be sent and summed in bfloat16 or wider, within the bound.
No kernel may reach another device: no remote copies, remote signals or barrier semaphores. Data moves between devices by JAX's collectives and lax.ppermute only.
A program may use at most 64 MiB of HBM per device.

```python
import math
import jax
import jax.numpy as jnp
import numpy as np
from jax import lax

D = 16384
HEADS = 128
KVH = 8
DH = 128
NSEQ = 4
CACHE_DEV = 2048
QTOK = 128
CACHE = 131072
N_BLK = 64


def shared_draw(key, pull):
    normal_keys = jax.random.normal(jax.random.fold_in(key, 11), (CACHE, KVH, DH), jnp.float32)
    keys = jnp.clip(normal_keys, -5.0, 5.0)
    base = jnp.clip(3.0 * jax.random.normal(jax.random.fold_in(key, 13), (QTOK, HEADS, DH), jnp.float32), -15.0, 15.0)
    row_scale = jnp.exp(jax.random.uniform(jax.random.fold_in(key, 14), (QTOK, 1, 1), jnp.float32, -0.69, 0.69))
    query_rows = base * (pull * row_scale + 1.0)
    tokens_hit = jax.random.randint(jax.random.fold_in(key, 15), (6,), 0, QTOK)
    heads_hit = jax.random.randint(jax.random.fold_in(key, 16), (6,), 0, HEADS)
    slots_hit = 2 * jax.random.randint(jax.random.fold_in(key, 17), (6,), 0, CACHE_DEV // 4 - 1)
    kv_hit = heads_hit // (HEADS // KVH)
    keys = keys.at[slots_hit + 1, kv_hit].set(keys[slots_hit + 1, kv_hit])
    query_rows = query_rows.at[tokens_hit, heads_hit].set(query_rows[tokens_hit, heads_hit])
    return (keys, query_rows)


def draw_cache_keys(key, part):
    pull = 0.0
    keys, query_rows = shared_draw(key, pull)
    return keys.astype(jnp.bfloat16)


def draw_queries(key, part):
    pull = 0.0
    keys, query_rows = shared_draw(key, pull)
    return query_rows.astype(jnp.bfloat16)


def set_ends(drawn, stream_key, least, top_value):
    index_at = [jax.random.randint(jax.random.fold_in(stream_key, axis), (), 0, length) for axis, length in enumerate(drawn.shape)]
    longest = drawn.shape.index(max(drawn.shape))
    beside = index_at[:longest] + [(index_at[longest] + 1) % drawn.shape[longest]] + index_at[longest + 1:]
    return drawn.at[tuple(index_at)].set(least).at[tuple(beside)].set(top_value)


def levels(own_key, dims, cuts, low, high):
    gain, own = 1.0, jax.random.fold_in(own_key, 6)
    for position, shards_of in cuts:
        steps = jnp.exp(jax.random.uniform(jax.random.fold_in(own, position), (shards_of,), jnp.float32, low / len(cuts), high / len(cuts)))
        gain = gain * jnp.repeat(steps, dims[position] // shards_of).reshape([-1 if axis == position else 1 for axis in range(len(dims))])
    return gain


def profile(count, total, most, lean):
    portions = [(1 << 20) // math.isqrt(grade ** lean) + 1 for grade in range(2, count + 1)]
    spare, counts = total - most - (count - 1), [1] * (count - 1)
    while spare > 0:
        free = [i for i in range(count - 1) if counts[i] < most]
        pool, budget = sum([portions[i] for i in free]), spare
        for i in free:
            more = min(most - counts[i], max(1, budget * portions[i] // pool), spare)
            counts[i] = counts[i] + more
            spare = spare - more
    return np.array([most] + counts)


def ragged_sizes(rng, number_of, total, most, skew):
    if number_of == 2:
        one = jax.random.randint(rng, (), max(1, total - most), min(most, total - 1) + 1)
        return jnp.stack([one, total - one])
    lengths = jnp.asarray(profile(number_of, total, most, skew), jnp.int32)
    couples = (number_of - 1) // 2
    source_of, sink = lengths[1:1 + 2 * couples:2], lengths[2:2 + 2 * couples:2]
    room = jnp.minimum(source_of - 1, most - sink)
    shifted = jax.random.randint(jax.random.fold_in(rng, 1), (couples,), 0, 1 << 20) % (room + 1)
    lengths = lengths.at[1:1 + 2 * couples:2].set(source_of - shifted).at[2:2 + 2 * couples:2].set(sink + shifted)
    return lengths[jax.random.permutation(jax.random.fold_in(rng, 2), number_of)]


def normal_values(stream_key, dims, width, reach, pieces=(), kind=jnp.bfloat16):
    values = width * jax.random.normal(stream_key, dims, jnp.float32)
    if pieces:
        values = values * levels(stream_key, dims, pieces, -0.22, 0.18)
    return jnp.clip(values, -reach, reach).astype(kind)


def setup_inputs(seed: int = 0) -> dict:
    streams_of = jax.random.split(jax.random.key(seed), 10)
    return {
        "queries": draw_queries(jax.random.fold_in(streams_of[9], 71), 0),
        "cache_keys": draw_cache_keys(jax.random.fold_in(streams_of[9], 71), 0),
        "cache_values": normal_values(streams_of[2], (CACHE, KVH, DH), 1.0, 6.0, ((0, 64), (1, 4))),
        "stretch_keys": normal_values(streams_of[3], (QTOK, KVH, DH), 2.5, 12.0, ((0, 64), (1, 4))),
        "stretch_values": normal_values(streams_of[4], (QTOK, KVH, DH), 1.0, 6.0, ((0, 64), (1, 4))),
        "valid_lens": set_ends(jax.random.randint(streams_of[5], (N_BLK,), CACHE_DEV // 2, CACHE_DEV + 1), jax.random.fold_in(streams_of[5], 1), CACHE_DEV // 2, CACHE_DEV).astype(jnp.int32),
        "offsets": set_ends(jax.random.randint(streams_of[6], (NSEQ,), CACHE // 2, CACHE + 1), jax.random.fold_in(streams_of[6], 1), CACHE // 2, CACHE).astype(jnp.int32),
        "seq_lengths": ragged_sizes(streams_of[7], NSEQ, QTOK, QTOK // 2, 2).astype(jnp.int32),
        "out_weight": normal_values(streams_of[8], (HEADS * DH, D), (HEADS * DH) ** -0.5, 0.046875, ((0, 4), (1, 64))),
    }


NEG = -1e30


def partial_block(query_group, keys, values, visible):
    scores = jnp.einsum("tjd,cd->tjc", query_group, keys.astype(jnp.float32)) * (DH ** -0.5)
    shown = visible[:, None, :]
    scores = jnp.where(shown, scores, NEG)
    top = jnp.max(scores, axis=-1)
    probs = jnp.where(shown, jnp.exp(scores - top[..., None]), 0.0)
    total = jnp.sum(probs, axis=-1)
    rounded = lax.optimization_barrier(probs.astype(jnp.bfloat16)).astype(jnp.float32)
    weighted = jnp.einsum("tjc,cd->tjd", rounded, values.astype(jnp.float32))
    return top, total, weighted


def combine(first, second):
    top = jnp.maximum(first[0], second[0])
    early = jnp.exp(first[0] - top)
    late = jnp.exp(second[0] - top)
    return (top, first[1] * early + second[1] * late, first[2] * early[..., None] + second[2] * late[..., None])


def reference(queries, cache_keys, cache_values, stretch_keys, stretch_values, valid_lens, offsets, seq_lengths, out_weight):
    group = HEADS // KVH
    tok_ids = jnp.arange(QTOK, dtype=jnp.int32)
    ends = jnp.cumsum(seq_lengths).astype(jnp.int32)
    which = jnp.sum((tok_ids[:, None] >= ends[None, :]).astype(jnp.int32), axis=1)
    limit = offsets[which]
    stretch_visible = (which[None, :] == which[:, None]) & (tok_ids[None, :] <= tok_ids[:, None])
    filled_all = jnp.arange(CACHE_DEV, dtype=jnp.int32)[None, :] < valid_lens[:, None]
    grouped = queries.reshape(QTOK, KVH, group, DH)

    def one_group(index):
        query_group = lax.dynamic_index_in_dim(grouped, index, 1, keepdims=False).astype(jnp.float32)
        key_group = lax.dynamic_index_in_dim(cache_keys, index, 1, keepdims=False).reshape(N_BLK, CACHE_DEV, DH)
        value_group = lax.dynamic_index_in_dim(cache_values, index, 1, keepdims=False).reshape(N_BLK, CACHE_DEV, DH)

        def step(carry, item):
            keys, values, filled, shard = item
            positions = shard * CACHE_DEV + jnp.arange(CACHE_DEV, dtype=jnp.int32)
            visible = (positions[None, :] < limit[:, None]) & filled[None, :]
            return combine(carry, partial_block(query_group, keys, values, visible)), None

        start = (jnp.full((QTOK, group), NEG, jnp.float32), jnp.zeros((QTOK, group), jnp.float32), jnp.zeros((QTOK, group, DH), jnp.float32))
        state, _ = lax.scan(step, start, (key_group, value_group, filled_all, jnp.arange(N_BLK, dtype=jnp.int32)))
        own_keys = lax.dynamic_index_in_dim(stretch_keys, index, 1, keepdims=False)
        own_values = lax.dynamic_index_in_dim(stretch_values, index, 1, keepdims=False)
        state = combine(state, partial_block(query_group, own_keys, own_values, stretch_visible))
        return state[2] / state[1][..., None]

    outputs = lax.map(one_group, jnp.arange(KVH, dtype=jnp.int32))
    attended = jnp.transpose(outputs, (1, 0, 2, 3)).reshape(QTOK, HEADS * DH).astype(jnp.bfloat16)
    return jnp.dot(attended, out_weight, preferred_element_type=jnp.float32).astype(jnp.bfloat16)
```

```python
import functools

import jax
import jax.numpy as jnp
from jax import lax
from jax.experimental import pallas as pl
from jax.experimental.pallas import tpu as pltpu
from jax.sharding import Mesh, PartitionSpec as P

NEG = -1e30
LOG2E = 1.4426950408889634
CHUNK = 8


def split3(x):
    hi = x.astype(jnp.bfloat16).astype(jnp.float32)
    rest = x - hi
    mid = rest.astype(jnp.bfloat16).astype(jnp.float32)
    low = (rest - mid).astype(jnp.bfloat16).astype(jnp.float32)
    return hi, mid, low


def seq_of(token, lens_ref, nseq):
    end = jnp.int32(0)
    which = jnp.zeros(token.shape, jnp.int32)
    for i in range(nseq):
        end = end + lens_ref[i]
        which = which + (token >= end).astype(jnp.int32)
    return which


def attend_kernel(
    other, nseq, offs_ref, lens_ref, valid_ref, q_ref, k_ref, v_ref, sk_ref, sv_ref, *rest
):
    if other:
        out_ref, kx_ref, vx_ref = rest
    else:
        got_ref, out_ref, kx_ref, vx_ref = rest
    kv, cache_dev, dh = k_ref.shape
    total = kx_ref.shape[1]
    z, x, c = lax.axis_index("z"), lax.axis_index("x"), lax.axis_index("c")
    me = (z * lax.axis_size("x") + x) * 2 + c
    tok_dev = sk_ref.shape[0]
    rows = q_ref.shape[2]
    group = rows // tok_dev

    @pl.when(pl.program_id(0) == 0)
    def _():
        pos = lax.broadcasted_iota(jnp.int32, (total, dh), 0)
        col = lax.broadcasted_iota(jnp.int32, (total, dh), 1)
        thr = jnp.zeros((total, dh), jnp.int32)
        for i in range(nseq):
            bound = jnp.minimum(valid_ref[0], offs_ref[i] - me * cache_dev)
            thr = jnp.where(col == i, bound, thr)
        own = (pos >= cache_dev) & (pos < cache_dev + tok_dev)
        hidden = (pos >= thr) & (col < nseq) & jnp.logical_not(own)
        bias = jnp.where(hidden, NEG, 0.0)
        bias = jnp.where(own & (col - nseq == pos - cache_dev), 1.0, bias)
        bias = bias.astype(jnp.bfloat16)
        pad = jnp.zeros((total - cache_dev - tok_dev, dh), jnp.float32)
        sk = sk_ref[...].astype(jnp.float32)
        sv = sv_ref[...].astype(jnp.float32)
        for h in range(kv):
            kx_ref[h, :cache_dev, :dh] = k_ref[h]
            kx_ref[h, cache_dev:, :dh] = jnp.concatenate([sk[:, h], pad], axis=0).astype(jnp.bfloat16)
            kx_ref[h, :, dh:] = bias
            vx_ref[h, :cache_dev, :dh] = v_ref[h]
            vx_ref[h, cache_dev:, :dh] = jnp.concatenate([sv[:, h], pad], axis=0).astype(jnp.bfloat16)
            vx_ref[h, :, dh:] = jnp.ones((total, dh), jnp.bfloat16)

    n = CHUNK * rows
    side = (1 - c) if other else c
    r = lax.broadcasted_iota(jnp.int32, (n, dh), 0)
    lane = lax.broadcasted_iota(jnp.int32, (n, dh), 1)
    place = pl.program_id(0) * CHUNK + r // rows
    token = (place * 2 + side) * tok_dev + (r % rows) // group
    seq = seq_of(token, lens_ref, nseq)
    feat = (lane == seq).astype(jnp.float32)
    for i in range(tok_dev):
        u = me * tok_dev + i
        useq = jnp.int32(0)
        end = jnp.int32(0)
        for s in range(nseq):
            end = end + lens_ref[s]
            useq = useq + (u >= end).astype(jnp.int32)
        seen = (seq == useq) & (u <= token)
        feat = jnp.where((lane == nseq + i) & jnp.logical_not(seen), NEG, feat)
    feat = feat.astype(jnp.bfloat16)
    scale = LOG2E * dh ** (-0.5)
    per = dh // rows
    stat = [jnp.zeros((8, dh), jnp.float32) for _ in range(CHUNK // per)]
    sub = lax.broadcasted_iota(jnp.int32, (8, dh), 0)
    diag = lax.broadcasted_iota(jnp.int32, (dh, dh), 0) == lax.broadcasted_iota(jnp.int32, (dh, dh), 1)
    for h in range(kv):
        q = q_ref[:, h].reshape(n, dh)
        qx = jnp.concatenate([q, feat], axis=1)
        s = lax.dot_general(
            qx, kx_ref[h], (((1,), (1,)), ((), ())), preferred_element_type=jnp.float32
        )
        top = jnp.max(s, axis=1, keepdims=True)
        p = jnp.exp2((s - top) * scale).astype(jnp.bfloat16)
        acc = jnp.dot(p, vx_ref[h], preferred_element_type=jnp.float32)
        total_l = acc[:, dh:]
        o = acc[:, :dh] / total_l
        lse = jnp.where(top > 0.5 * NEG, top * scale + jnp.log2(total_l), NEG)
        if not other:
            for g in range(CHUNK // per):
                back = got_ref[g * per, 2 * rows :, :].astype(jnp.float32)
                line = back[3 * h : 3 * h + 1] + back[3 * h + 1 : 3 * h + 2] + back[3 * h + 2 : 3 * h + 3]
                theirs = jnp.sum(jnp.where(diag, line, 0.0), axis=1, keepdims=True)
                mine = lse[g * dh : (g + 1) * dh]
                high = jnp.maximum(mine, theirs)
                a, b = jnp.exp2(mine - high), jnp.exp2(theirs - high)
                both = a + b
                o_theirs = got_ref[g * per : (g + 1) * per, h * rows : (h + 1) * rows, :]
                o_theirs = o_theirs.reshape(dh, dh).astype(jnp.float32)
                mixed = (o[g * dh : (g + 1) * dh] * a + o_theirs * b) / both
                out_ref[g * per : (g + 1) * per, h * rows : (h + 1) * rows, :] = mixed.reshape(per, rows, dh).astype(jnp.bfloat16)
                line = jnp.sum(jnp.where(diag, high + jnp.log2(both), 0.0), axis=0, keepdims=True)
                for i, part in enumerate(split3(line)):
                    stat[g] = jnp.where(sub == 3 * h + i, part, stat[g])
        else:
            out_ref[:, h * rows : (h + 1) * rows, :] = o.reshape(CHUNK, rows, dh).astype(jnp.bfloat16)
            for g in range(CHUNK // per):
                line = jnp.sum(jnp.where(diag, lse[g * dh : (g + 1) * dh], 0.0), axis=0, keepdims=True)
                for i, part in enumerate(split3(line)):
                    stat[g] = jnp.where(sub == 3 * h + i, part, stat[g])
    for g in range(CHUNK // per):
        for i in range(per):
            out_ref[g * per + i, 2 * rows :, :] = stat[g].astype(jnp.bfloat16)


def attend(other, nseq, offs, lens, valid, q, k, v, sk, sv, got=None):
    count, kv, rows, dh = q.shape
    cache_dev = k.shape[1]
    total = cache_dev + dh
    smem = pl.BlockSpec(memory_space=pltpu.SMEM)
    whole = lambda a: pl.BlockSpec(a.shape, lambda i: (0,) * a.ndim)
    out_rows = kv * rows + 8
    out_block = pl.BlockSpec((CHUNK, out_rows, dh), lambda i: (i, 0, 0))
    operands = [offs, lens, valid, q, k, v, sk, sv]
    specs = [smem, smem, smem, pl.BlockSpec((CHUNK, kv, rows, dh), lambda i: (i, 0, 0, 0)), whole(k), whole(v), whole(sk), whole(sv)]
    if got is not None:
        operands.append(got)
        specs.append(out_block)
    all_rows = count * kv * rows
    return pl.pallas_call(
        functools.partial(attend_kernel, other, nseq),
        grid=(count // CHUNK,),
        in_specs=specs,
        out_specs=out_block,
        out_shape=jax.ShapeDtypeStruct((count, out_rows, dh), jnp.bfloat16),
        scratch_shapes=[
            pltpu.VMEM((kv, total, 2 * dh), jnp.bfloat16),
            pltpu.VMEM((kv, total, 2 * dh), jnp.bfloat16),
        ],
        compiler_params=pltpu.CompilerParams(vmem_limit_bytes=48 * 2**20),
        cost_estimate=pl.CostEstimate(
            flops=4 * all_rows * total * 2 * dh, bytes_accessed=4 * 2**20, transcendentals=all_rows * total
        ),
    )(*operands)


def merge_kernel(rows, in_ref, out_ref, flat_ref):
    count, _, dh = in_ref.shape
    kv = 2
    x = lax.axis_index("x")
    lane = lax.broadcasted_iota(jnp.int32, (1, dh), 1)
    lines = []
    for h in range(kv):
        parts = []
        for i in range(count):
            block = in_ref[i, kv * rows :, :].astype(jnp.float32)
            parts.append(block[3 * h : 3 * h + 1] + block[3 * h + 1 : 3 * h + 2] + block[3 * h + 2 : 3 * h + 3])
        lines.append(jnp.concatenate(parts, axis=0))
    for h in range(kv):
        lse = lines[h]
        high = jnp.max(lse, axis=0, keepdims=True)
        w = jnp.exp2(lse - high)
        w = w / jnp.sum(w, axis=0, keepdims=True)
        w = jnp.concatenate([w, jnp.zeros((dh - count, dh), jnp.float32)], axis=0)
        wt = w.T
        mine = jnp.zeros((rows, dh), jnp.float32)
        for i in range(dh // rows):
            mine = jnp.where(x == i, wt[i * rows : (i + 1) * rows], mine)
        acc = jnp.zeros((rows, dh), jnp.float32)
        for i in range(count):
            acc = acc + mine[:, i : i + 1] * in_ref[i, h * rows : (h + 1) * rows, :].astype(jnp.float32)
        group = rows // 2
        for t in range(2):
            for j in range(group):
                at = (h * group + j) * dh
                flat_ref[t : t + 1, at : at + dh] = acc[t * group + j : t * group + j + 1]
    value = flat_ref[...].astype(jnp.bfloat16)
    for i in range(count):
        out_ref[i] = value


def merge(got, rows):
    count, _, dh = got.shape
    width = 2 * rows // 2 * dh
    return pl.pallas_call(
        functools.partial(merge_kernel, rows),
        out_shape=jax.ShapeDtypeStruct((count, 2, width), jnp.bfloat16),
        in_specs=[pl.BlockSpec(memory_space=pltpu.VMEM)],
        out_specs=pl.BlockSpec(memory_space=pltpu.VMEM),
        scratch_shapes=[pltpu.VMEM((2, width), jnp.float32)],
        compiler_params=pltpu.CompilerParams(vmem_limit_bytes=32 * 2**20),
    )(got)


def body(queries, cache_keys, cache_values, stretch_keys, stretch_values, valid_lens, offsets, seq_lengths, out_weight):
    tok_dev, heads, dh = queries.shape
    kv = cache_keys.shape[1]
    group = heads // kv
    nseq = seq_lengths.shape[0]
    count = lax.axis_size("z") * lax.axis_size("x")
    rows = tok_dev * group
    c = lax.axis_index("c")
    zx = ("z", "x")
    swap = lambda a: lax.ppermute(a, "c", [(0, 1), (1, 0)])
    everywhere = lambda a: lax.all_to_all(a, zx, 0, 0, tiled=True)

    packed = queries.reshape(tok_dev, kv, group, dh).transpose(1, 0, 2, 3).reshape(kv, rows, dh)
    mine = everywhere(jnp.broadcast_to(packed[None], (count, kv, rows, dh)))
    theirs = swap(mine)
    keys = cache_keys.transpose(1, 0, 2)
    values = cache_values.transpose(1, 0, 2)
    shared = (nseq, offsets, seq_lengths, valid_lens)
    away = attend(True, *shared, theirs, keys, values, stretch_keys, stretch_values)
    part = attend(False, *shared, mine, keys, values, stretch_keys, stretch_values, swap(away))
    attended = everywhere(merge(everywhere(part), rows))
    attended_other = swap(attended)
    width = attended.shape[-1]
    project = lambda a: jnp.dot(a.reshape(count * tok_dev, width), out_weight, preferred_element_type=jnp.float32)
    near, far = project(attended), project(attended_other)
    ways = lax.axis_size("head")
    cols = out_weight.shape[1]
    terms = jnp.stack([a.reshape(ways, count // ways, tok_dev, cols) for a in (near, far)], axis=1)
    terms = jnp.sum(lax.all_to_all(terms, "head", 0, 0, tiled=True), axis=0)
    first = jnp.where(c == 0, terms[0], terms[1])
    second = jnp.where(c == 0, terms[1], terms[0])
    return jnp.stack([first, second], axis=1).reshape(-1, cols).astype(jnp.bfloat16)


def solution(mesh):
    grid = Mesh(mesh.devices.reshape(8, 4, 2, 4), ("z", "x", "c", "head"))
    blk = ("z", "x", "c")
    return jax.shard_map(
        body,
        mesh=grid,
        in_specs=(
            P(blk, "head", None),
            P(blk, "head", None),
            P(blk, "head", None),
            P(blk, "head", None),
            P(blk, "head", None),
            P(blk),
            P(),
            P(),
            P("head", blk),
        ),
        out_specs=P("head", blk),
        check_vma=False,
    )
```

```python
import functools

import jax
import jax.numpy as jnp
from jax import lax
from jax.experimental import pallas as pl
from jax.experimental.pallas import tpu as pltpu
from jax.sharding import Mesh, PartitionSpec as P

NEG = -1e30
LOG2E = 1.4426950408889634


def split3(x):
    hi = x.astype(jnp.bfloat16).astype(jnp.float32)
    rest = x - hi
    mid = rest.astype(jnp.bfloat16).astype(jnp.float32)
    low = (rest - mid).astype(jnp.bfloat16).astype(jnp.float32)
    return hi, mid, low


def seq_of(token, lens_ref, nseq):
    end = jnp.int32(0)
    which = jnp.zeros(token.shape, jnp.int32)
    for i in range(nseq):
        end = end + lens_ref[i]
        which = which + (token >= end).astype(jnp.int32)
    return which


def prepare_kernel(nseq, offs_ref, lens_ref, valid_ref, k_ref, v_ref, sk_ref, sv_ref, kx_ref, vx_ref, feat_ref):
    kv, cache_dev, dh = k_ref.shape
    total = vx_ref.shape[1]
    tok_dev = sk_ref.shape[0]
    z, x, c = lax.axis_index("z"), lax.axis_index("x"), lax.axis_index("c")
    me = (z * lax.axis_size("x") + x) * 2 + c
    pos = lax.broadcasted_iota(jnp.int32, (dh, cache_dev), 1)
    row = lax.broadcasted_iota(jnp.int32, (dh, 1), 0)
    thr = jnp.full((dh, 1), total, jnp.int32)
    for i in range(nseq):
        bound = jnp.minimum(valid_ref[0], offs_ref[i] - me * cache_dev)
        thr = jnp.where(row == i, bound, thr)
    bias = jnp.where(pos >= thr, NEG, 0.0).astype(jnp.bfloat16)
    tail_pos = lax.broadcasted_iota(jnp.int32, (dh, dh), 1)
    tail_row = lax.broadcasted_iota(jnp.int32, (dh, dh), 0)
    tail = jnp.where((tail_pos >= tok_dev) & (tail_row < nseq), NEG, 0.0)
    tail = jnp.where((tail_pos < tok_dev) & (tail_row == nseq + tail_pos), 1.0, tail).astype(jnp.bfloat16)
    pad = jnp.zeros((dh - tok_dev, dh), jnp.float32)
    sk = sk_ref[...].astype(jnp.float32)
    sv = sv_ref[...].astype(jnp.float32)
    for h in range(kv):
        kx_ref[h, :dh, :cache_dev] = k_ref[h].T
        kx_ref[h, :dh, cache_dev:] = jnp.concatenate([sk[:, h], pad], axis=0).T.astype(jnp.bfloat16)
        kx_ref[h, dh:, :cache_dev] = bias
        kx_ref[h, dh:, cache_dev:] = tail
        vx_ref[h, :cache_dev, :dh] = v_ref[h]
        vx_ref[h, cache_dev:, :dh] = jnp.concatenate([sv[:, h], pad], axis=0).astype(jnp.bfloat16)
        vx_ref[h, :, dh:] = jnp.ones((total, dh), jnp.bfloat16)
    sides, ways, tile, _ = feat_ref.shape
    toks = tile // GROUP
    r = lax.broadcasted_iota(jnp.int32, (toks, dh), 0)
    lane = lax.broadcasted_iota(jnp.int32, (toks, dh), 1)
    for side in range(sides):
        core = c if side == 0 else 1 - c
        for d in range(ways):
            place = r // tok_dev * ways + (x ^ d)
            token = (place * 2 + core) * tok_dev + r % tok_dev
            seq = seq_of(token, lens_ref, nseq)
            feat = (lane == seq).astype(jnp.float32)
            for i in range(tok_dev):
                u = me * tok_dev + i
                useq = jnp.int32(0)
                end = jnp.int32(0)
                for n in range(nseq):
                    end = end + lens_ref[n]
                    useq = useq + (u >= end).astype(jnp.int32)
                seen = (seq == useq) & (u <= token)
                feat = jnp.where((lane == nseq + i) & jnp.logical_not(seen), NEG, feat)
            feat = jnp.broadcast_to(feat[:, None, :], (toks, GROUP, dh)).reshape(tile, dh)
            feat_ref[side, d] = feat.astype(jnp.bfloat16)


GROUP = 16
VMEM = pl.BlockSpec(memory_space=pltpu.VMEM)
SMEM = pl.BlockSpec(memory_space=pltpu.SMEM)


def prepare(offs, lens, valid, k, v, sk, sv, ways, tile):
    kv, cache_dev, dh = k.shape
    total = cache_dev + dh
    keys = jax.ShapeDtypeStruct((kv, 2 * dh, total), jnp.bfloat16)
    values = jax.ShapeDtypeStruct((kv, total, 2 * dh), jnp.bfloat16)
    return pl.pallas_call(
        functools.partial(prepare_kernel, offs.shape[0]),
        in_specs=[SMEM] * 3 + [VMEM] * 4,
        out_specs=[VMEM] * 3,
        out_shape=[keys, values, jax.ShapeDtypeStruct((2, ways, tile, dh), jnp.bfloat16)],
        compiler_params=pltpu.CompilerParams(vmem_limit_bytes=16 * 2**20),
        cost_estimate=pl.CostEstimate(flops=2 * kv * total * dh * 8, bytes_accessed=8 * 2**20, transcendentals=0),
    )(offs, lens, valid, k, v, sk, sv)


def stat_block(lines, dh):
    sub = lax.broadcasted_iota(jnp.int32, (8, dh), 0)
    stat = jnp.zeros((8, dh), jnp.float32)
    for h, line in enumerate(lines):
        for i, part in enumerate(split3(line)):
            stat = jnp.where(sub == 3 * h + i, part, stat)
    return stat.astype(jnp.bfloat16)


def line_of(block, h):
    block = block.astype(jnp.float32)
    return block[3 * h : 3 * h + 1] + block[3 * h + 1 : 3 * h + 2] + block[3 * h + 2 : 3 * h + 3]


def rows_of(ref, at, g, h, tok_dev, heads, group, dh):
    per = dh // (tok_dev * group)
    where = pl.ds(g * per, per)
    parts = [ref[(*at, where, pl.ds(t * heads + h * group, group), slice(None))] for t in range(tok_dev)]
    return jnp.stack(parts, axis=1).reshape(dh, dh).astype(jnp.float32)


def attend_kernel(jobs, n_q, merging, *refs):
    q_refs = refs[:n_q]
    feat_ref, kx_ref, vx_ref = refs[n_q : n_q + 3]
    rest = refs[n_q + 3 :]
    if merging:
        own_ref, got_own_ref, got_ref, out_ref = rest[:4]
        outs, rest = [out_ref], rest[4:]
    else:
        n_out = 1 + max(job[3] for job in jobs)
        outs, rest = list(rest[:n_out]), rest[n_out:]
    sa_ref, sb_ref = rest
    count, tok_dev, heads, dh = q_refs[0].shape
    kv, _, total = kx_ref.shape
    group = heads // kv
    n = count * tok_dev * group
    per = dh // (tok_dev * group)
    groups = n // dh
    scale = LOG2E * dh ** (-0.5)
    edges = [0, 512, 1024, 1536, total]
    spans = list(zip(edges[:-1], edges[1:]))
    diag = lax.broadcasted_iota(jnp.int32, (dh, dh), 0) == lax.broadcasted_iota(jnp.int32, (dh, dh), 1)
    x = lax.axis_index("x")

    def load(job, h):
        q = q_refs[job[0]][:, :, h * group : (h + 1) * group, :].reshape(n, dh)
        return jnp.concatenate([q, feat_ref[job[1], job[2]]], axis=1)

    def score(qx, h, s_ref, span, top):
        s = jnp.dot(qx, kx_ref[h, :, span[0] : span[1]], preferred_element_type=jnp.float32)
        s_ref[:, span[0] : span[1]] = s
        for i in range((span[1] - span[0]) // dh):
            part = s[:, i * dh : (i + 1) * dh]
            top = part if top is None else jnp.maximum(top, part)
        return top

    def merge_pair(value, mine, o_theirs, theirs):
        high = jnp.maximum(mine, theirs)
        a, b = jnp.exp2(mine - high), jnp.exp2(theirs - high)
        both = a + b
        return (value * a + o_theirs * b) / both, high + jnp.log2(both)

    def column(line):
        return jnp.sum(jnp.where(diag, line, 0.0), axis=1, keepdims=True)

    def put(job, g, h, value):
        value = value.reshape(per, tok_dev, group, dh).astype(jnp.bfloat16)
        for t in range(tok_dev):
            place = pl.ds(t * heads + h * group, group)
            if merging:
                outs[0][pl.ds(g * per, per), x ^ job[2], place, :] = value[:, t]
            else:
                outs[job[3]][(*job[4], pl.ds(g * per, per), place, slice(None))] = value[:, t]

    def put_stat(job, g, lines):
        stat = stat_block(lines, dh)
        for i in range(per):
            if merging:
                outs[0][g * per + i, x ^ job[2], tok_dev * heads :, :] = stat
            else:
                outs[job[3]][(*job[4], g * per + i, slice(tok_dev * heads, None), slice(None))] = stat

    def half(job, h, s_ref, lanes_top, later):
        top = jnp.max(lanes_top, axis=1, keepdims=True)
        acc = None
        next_top = None
        if later is not None:
            next_qx, next_h, next_ref = load(*later[:2]), later[1], later[2]
        for span in spans:
            if later is not None:
                next_top = score(next_qx, next_h, next_ref, span, next_top)
            p = jnp.exp2((s_ref[:, span[0] : span[1]] - top) * scale).astype(jnp.bfloat16)
            term = jnp.dot(p, vx_ref[h, span[0] : span[1], :], preferred_element_type=jnp.float32)
            acc = term if acc is None else acc + term
        total_l = acc[:, dh:]
        o = acc[:, :dh] / total_l
        lse = jnp.where(top > 0.5 * NEG, top * scale + jnp.log2(total_l), NEG)
        lines = []
        for g in range(groups):
            mine = lse[g * dh : (g + 1) * dh]
            value = o[g * dh : (g + 1) * dh]
            if merging:
                theirs = column(line_of(got_ref[job[2] - 1, g * per, tok_dev * heads :, :], h))
                o_theirs = rows_of(got_ref, (job[2] - 1,), g, h, tok_dev, heads, group, dh)
                value, mine = merge_pair(value, mine, o_theirs, theirs)
            put(job, g, h, value)
            lines.append(jnp.sum(jnp.where(diag, mine, 0.0), axis=0, keepdims=True))
        return lines, next_top

    first = load(jobs[0], 0)
    top = None
    for span in spans:
        top = score(first, 0, sa_ref, span, top)
    if merging:
        for g in range(groups):
            lines = []
            for h in range(kv):
                at = (g * per, slice(tok_dev * heads, None), slice(None))
                lse = [column(line_of(ref[at], h)) for ref in (own_ref, got_own_ref)]
                o = [rows_of(ref, (), g, h, tok_dev, heads, group, dh) for ref in (own_ref, got_own_ref)]
                value, mine = merge_pair(o[0], lse[0], o[1], lse[1])
                put((0, 0, 0), g, h, value)
                mine = jnp.broadcast_to(mine, (dh, dh))
                lines.append(jnp.sum(jnp.where(diag, mine, 0.0), axis=0, keepdims=True))
            put_stat((0, 0, 0), g, lines)
    for i, job in enumerate(jobs):
        lines_a, top = half(job, 0, sa_ref, top, (job, 1, sb_ref))
        later = (jobs[i + 1], 0, sa_ref) if i + 1 < len(jobs) else None
        lines_b, top = half(job, 1, sb_ref, top, later)
        for g in range(groups):
            put_stat(job, g, (lines_a[g], lines_b[g]))


def attend(jobs, queries, feat, kx, vx, out_shapes, merge_with=()):
    count, tok_dev, heads, dh = queries[0].shape
    kv, _, total = kx.shape
    n = count * tok_dev * heads // kv
    work = n * kv * len(jobs) * total
    shapes = [jax.ShapeDtypeStruct(shape, jnp.bfloat16) for shape in out_shapes]
    return pl.pallas_call(
        functools.partial(attend_kernel, jobs, len(queries), bool(merge_with)),
        in_specs=[VMEM] * (len(queries) + 3 + len(merge_with)),
        out_specs=[VMEM] * len(shapes),
        out_shape=shapes,
        scratch_shapes=[
            pltpu.VMEM((n, total), jnp.float32),
            pltpu.VMEM((n, total), jnp.float32),
        ],
        compiler_params=pltpu.CompilerParams(vmem_limit_bytes=26 * 2**20),
        cost_estimate=pl.CostEstimate(flops=8 * work * dh, bytes_accessed=5 * 2**20, transcendentals=work),
    )(*queries, feat, kx, vx, *merge_with)


def replicate_kernel(in_ref, out_ref):
    value = in_ref[...]
    for i in range(out_ref.shape[0]):
        out_ref[i] = value


def replicate(a, count):
    return pl.pallas_call(
        replicate_kernel,
        in_specs=[VMEM],
        out_specs=VMEM,
        out_shape=jax.ShapeDtypeStruct((count,) + a.shape, a.dtype),
    )(a)


def merge_kernel(rows, in_ref, out_ref, flat_ref):
    count, _, dh = in_ref.shape
    kv = 2
    z = lax.axis_index("z")
    lines = []
    for h in range(kv):
        parts = []
        for i in range(count):
            block = in_ref[i, kv * rows :, :].astype(jnp.float32)
            parts.append(block[3 * h : 3 * h + 1] + block[3 * h + 1 : 3 * h + 2] + block[3 * h + 2 : 3 * h + 3])
        lines.append(jnp.concatenate(parts, axis=0))
    for h in range(kv):
        lse = lines[h]
        high = jnp.max(lse, axis=0, keepdims=True)
        w = jnp.exp2(lse - high)
        w = w / jnp.sum(w, axis=0, keepdims=True)
        w = jnp.concatenate([w, jnp.zeros((dh - count, dh), jnp.float32)], axis=0)
        wt = w.T
        mine = jnp.zeros((rows, dh), jnp.float32)
        for i in range(dh // rows):
            mine = jnp.where(z % (dh // rows) == i, wt[i * rows : (i + 1) * rows], mine)
        group = rows // 2
        acc = jnp.zeros((rows, dh), jnp.float32)
        for i in range(count):
            blocks = [in_ref[i, t * 2 * group + h * group : t * 2 * group + (h + 1) * group, :] for t in range(2)]
            acc = acc + mine[:, i : i + 1] * jnp.concatenate(blocks, axis=0).astype(jnp.float32)
        for t in range(2):
            for j in range(group):
                at = (h * group + j) * dh
                flat_ref[t : t + 1, at : at + dh] = acc[t * group + j : t * group + j + 1]
    value = flat_ref[...].astype(jnp.bfloat16)
    for i in range(count):
        out_ref[i] = value


def merge(got, rows):
    count, _, dh = got.shape
    width = 2 * rows // 2 * dh
    return pl.pallas_call(
        functools.partial(merge_kernel, rows),
        out_shape=jax.ShapeDtypeStruct((count, 2, width), jnp.bfloat16),
        in_specs=[pl.BlockSpec(memory_space=pltpu.VMEM)],
        out_specs=pl.BlockSpec(memory_space=pltpu.VMEM),
        scratch_shapes=[pltpu.VMEM((2, width), jnp.float32)],
        compiler_params=pltpu.CompilerParams(vmem_limit_bytes=16 * 2**20),
    )(got)


def body(queries, cache_keys, cache_values, stretch_keys, stretch_values, valid_lens, offsets, seq_lengths, out_weight):
    tok_dev, heads, dh = queries.shape
    kv = cache_keys.shape[1]
    group = heads // kv
    count = lax.axis_size("z") * lax.axis_size("x")
    rows = tok_dev * group
    c = lax.axis_index("c")
    zx = ("z", "x")
    swap = lambda a: lax.ppermute(a, "c", [(0, 1), (1, 0)])
    everywhere = lambda a: lax.all_to_all(a, zx, 0, 0, tiled=True)

    deep, ways = lax.axis_size("z"), lax.axis_size("x")
    tile = deep * rows
    mine = [lax.all_to_all(replicate(queries, deep), "z", 0, 0, tiled=True)]
    keys = cache_keys.transpose(1, 0, 2)
    values = cache_values.transpose(1, 0, 2)
    mine[0], keys, values = lax.optimization_barrier((mine[0], keys, values))
    kx, vx, feat = prepare(offsets, seq_lengths, valid_lens, keys, values, stretch_keys, stretch_values, ways, tile)
    theirs = [swap(mine[0])]
    for d in range(1, ways):
        mine.append(lax.ppermute(mine[0], "x", [(i, i ^ d) for i in range(ways)]))
    block = (deep, tok_dev * heads + 8, dh)
    jobs = [(1, 1, 0, 0, ()), (0, 0, 0, 1, ())]
    away_near, near = attend(jobs, [mine[0], theirs[0]], feat, kx, vx, [block, block])
    *mine[1:], near = lax.optimization_barrier((*mine[1:], near))
    for d in range(1, ways):
        theirs.append(swap(mine[d]))
    jobs = [(d - 1, 1, d, 0, (d - 1,)) for d in range(1, ways)]
    (away,) = attend(jobs, theirs[1:], feat, kx, vx, [(ways - 1,) + block])
    jobs = [(d - 1, 0, d, 0, ()) for d in range(1, ways)]
    merge_with = (near, swap(away_near), swap(away))
    (part,) = attend(jobs, mine[1:], feat, kx, vx, [(deep, ways) + block[1:]], merge_with)
    part = part.reshape((count,) + block[1:])
    attended = everywhere(merge(everywhere(part), rows))
    attended_other = swap(attended)
    width = attended.shape[-1]
    project = lambda a: jnp.dot(a.reshape(count * tok_dev, width), out_weight, preferred_element_type=jnp.float32)
    near, far = project(attended), project(attended_other)
    ways = lax.axis_size("head")
    cols = out_weight.shape[1]
    terms = jnp.stack([a.reshape(ways, count // ways, tok_dev, cols) for a in (near, far)], axis=1)
    y = lax.axis_index("head")
    piece = lambda d: lax.dynamic_index_in_dim(terms, y ^ d, 0, keepdims=False)
    total = piece(0)
    for d in range(1, ways):
        total = total + lax.ppermute(piece(d), "head", [(i, i ^ d) for i in range(ways)])
    terms = total
    first = jnp.where(c == 0, terms[0], terms[1])
    second = jnp.where(c == 0, terms[1], terms[0])
    return jnp.stack([first, second], axis=1).reshape(-1, cols).astype(jnp.bfloat16)


def solution(mesh):
    grid = Mesh(mesh.devices.reshape(8, 4, 2, 4), ("z", "x", "c", "head"))
    blk = ("z", "x", "c")
    return jax.shard_map(
        body,
        mesh=grid,
        in_specs=(
            P(blk, "head", None),
            P(blk, "head", None),
            P(blk, "head", None),
            P(blk, "head", None),
            P(blk, "head", None),
            P(blk),
            P(),
            P(),
            P("head", blk),
        ),
        out_specs=P("head", blk),
        check_vma=False,
    )
```

```python
import functools

import jax
import jax.numpy as jnp
from jax import lax
from jax.experimental import pallas as pl
from jax.experimental.pallas import tpu as pltpu
from jax.sharding import Mesh, PartitionSpec as P

NEG = -1e30
LOG2E = 1.4426950408889634


def split3(x):
    hi = x.astype(jnp.bfloat16).astype(jnp.float32)
    rest = x - hi
    mid = rest.astype(jnp.bfloat16).astype(jnp.float32)
    low = (rest - mid).astype(jnp.bfloat16).astype(jnp.float32)
    return hi, mid, low


def seq_of(token, lens_ref, nseq):
    end = jnp.int32(0)
    which = jnp.zeros(token.shape, jnp.int32)
    for i in range(nseq):
        end = end + lens_ref[i]
        which = which + (token >= end).astype(jnp.int32)
    return which


def prepare_kernel(nseq, offs_ref, lens_ref, valid_ref, k_ref, v_ref, sk_ref, sv_ref, kx_ref, vx_ref, feat_ref):
    kv, cache_dev, dh = k_ref.shape
    total = vx_ref.shape[1]
    tok_dev = sk_ref.shape[0]
    z, x, c = lax.axis_index("z"), lax.axis_index("x"), lax.axis_index("c")
    me = (z * lax.axis_size("x") + x) * 2 + c
    pos = lax.broadcasted_iota(jnp.int32, (dh, cache_dev), 1)
    row = lax.broadcasted_iota(jnp.int32, (dh, 1), 0)
    thr = jnp.full((dh, 1), total, jnp.int32)
    for i in range(nseq):
        bound = jnp.minimum(valid_ref[0], offs_ref[i] - me * cache_dev)
        thr = jnp.where(row == i, bound, thr)
    bias = jnp.where(pos >= thr, NEG, 0.0).astype(jnp.bfloat16)
    tail_pos = lax.broadcasted_iota(jnp.int32, (dh, dh), 1)
    tail_row = lax.broadcasted_iota(jnp.int32, (dh, dh), 0)
    tail = jnp.where((tail_pos >= tok_dev) & (tail_row < nseq), NEG, 0.0)
    tail = jnp.where((tail_pos < tok_dev) & (tail_row == nseq + tail_pos), 1.0, tail).astype(jnp.bfloat16)
    pad = jnp.zeros((dh - tok_dev, dh), jnp.float32)
    sk = sk_ref[...].astype(jnp.float32)
    sv = sv_ref[...].astype(jnp.float32)
    for h in range(kv):
        kx_ref[h, :dh, :cache_dev] = k_ref[h].T
        kx_ref[h, :dh, cache_dev:] = jnp.concatenate([sk[:, h], pad], axis=0).T.astype(jnp.bfloat16)
        kx_ref[h, dh:, :cache_dev] = bias
        kx_ref[h, dh:, cache_dev:] = tail
        vx_ref[h, :cache_dev, :dh] = v_ref[h]
        vx_ref[h, cache_dev:, :dh] = jnp.concatenate([sv[:, h], pad], axis=0).astype(jnp.bfloat16)
        vx_ref[h, :, dh:] = jnp.ones((total, dh), jnp.bfloat16)
    sides, ways, tile, _ = feat_ref.shape
    toks = tile // GROUP
    r = lax.broadcasted_iota(jnp.int32, (toks, dh), 0)
    lane = lax.broadcasted_iota(jnp.int32, (toks, dh), 1)
    for side in range(sides):
        core = c if side == 0 else 1 - c
        for d in range(ways):
            place = r // tok_dev * ways + (x ^ d)
            token = (place * 2 + core) * tok_dev + r % tok_dev
            seq = seq_of(token, lens_ref, nseq)
            feat = (lane == seq).astype(jnp.float32)
            for i in range(tok_dev):
                u = me * tok_dev + i
                useq = jnp.int32(0)
                end = jnp.int32(0)
                for n in range(nseq):
                    end = end + lens_ref[n]
                    useq = useq + (u >= end).astype(jnp.int32)
                seen = (seq == useq) & (u <= token)
                feat = jnp.where((lane == nseq + i) & jnp.logical_not(seen), NEG, feat)
            feat = jnp.broadcast_to(feat[:, None, :], (toks, GROUP, dh)).reshape(tile, dh)
            feat_ref[side, d] = feat.astype(jnp.bfloat16)


GROUP = 16
VMEM = pl.BlockSpec(memory_space=pltpu.VMEM)
SMEM = pl.BlockSpec(memory_space=pltpu.SMEM)


def prepare(offs, lens, valid, k, v, sk, sv, ways, tile):
    kv, cache_dev, dh = k.shape
    total = cache_dev + dh
    keys = jax.ShapeDtypeStruct((kv, 2 * dh, total), jnp.bfloat16)
    values = jax.ShapeDtypeStruct((kv, total, 2 * dh), jnp.bfloat16)
    return pl.pallas_call(
        functools.partial(prepare_kernel, offs.shape[0]),
        in_specs=[SMEM] * 3 + [VMEM] * 4,
        out_specs=[VMEM] * 3,
        out_shape=[keys, values, jax.ShapeDtypeStruct((2, ways, tile, dh), jnp.bfloat16)],
        compiler_params=pltpu.CompilerParams(vmem_limit_bytes=16 * 2**20),
        cost_estimate=pl.CostEstimate(flops=2 * kv * total * dh * 8, bytes_accessed=8 * 2**20, transcendentals=0),
    )(offs, lens, valid, k, v, sk, sv)


def stat_block(lines, dh):
    sub = lax.broadcasted_iota(jnp.int32, (8, dh), 0)
    stat = jnp.zeros((8, dh), jnp.float32)
    for h, line in enumerate(lines):
        for i, part in enumerate(split3(line)):
            stat = jnp.where(sub == 3 * h + i, part, stat)
    return stat.astype(jnp.bfloat16)


def line_of(block, h):
    block = block.astype(jnp.float32)
    return block[3 * h : 3 * h + 1] + block[3 * h + 1 : 3 * h + 2] + block[3 * h + 2 : 3 * h + 3]


def rows_of(ref, at, g, h, tok_dev, heads, group, dh):
    per = dh // (tok_dev * group)
    where = pl.ds(g * per, per)
    parts = [ref[(*at, where, pl.ds(t * heads + h * group, group), slice(None))] for t in range(tok_dev)]
    return jnp.stack(parts, axis=1).reshape(dh, dh).astype(jnp.float32)


def attend_kernel(jobs, n_q, merging, *refs):
    q_refs = refs[:n_q]
    feat_ref, kx_ref, vx_ref = refs[n_q : n_q + 3]
    rest = refs[n_q + 3 :]
    if merging:
        own_ref, got_ref, out_ref = rest[:3]
        outs, rest = [out_ref], rest[3:]
    else:
        n_out = 1 + max(job[3] for job in jobs)
        outs, rest = list(rest[:n_out]), rest[n_out:]
    sa_ref, sb_ref = rest
    count, tok_dev, heads, dh = q_refs[0].shape
    kv, _, total = kx_ref.shape
    group = heads // kv
    n = count * tok_dev * group
    per = dh // (tok_dev * group)
    groups = n // dh
    scale = LOG2E * dh ** (-0.5)
    edges = [0, 512, 1024, 1536, total]
    spans = list(zip(edges[:-1], edges[1:]))
    diag = lax.broadcasted_iota(jnp.int32, (dh, dh), 0) == lax.broadcasted_iota(jnp.int32, (dh, dh), 1)
    x = lax.axis_index("x")

    def load(job, h):
        q = q_refs[job[0]][:, :, h * group : (h + 1) * group, :].reshape(n, dh)
        return jnp.concatenate([q, feat_ref[job[1], job[2]]], axis=1)

    def score(qx, h, s_ref, span, top):
        s = jnp.dot(qx, kx_ref[h, :, span[0] : span[1]], preferred_element_type=jnp.float32)
        s_ref[:, span[0] : span[1]] = s
        for i in range((span[1] - span[0]) // dh):
            part = s[:, i * dh : (i + 1) * dh]
            top = part if top is None else jnp.maximum(top, part)
        return top

    def merge_pair(value, mine, o_theirs, theirs):
        high = jnp.maximum(mine, theirs)
        a, b = jnp.exp2(mine - high), jnp.exp2(theirs - high)
        both = a + b
        return (value * a + o_theirs * b) / both, high + jnp.log2(both)

    def column(line):
        return jnp.sum(jnp.where(diag, line, 0.0), axis=1, keepdims=True)

    def put(job, g, h, value):
        value = value.reshape(per, tok_dev, group, dh).astype(jnp.bfloat16)
        for t in range(tok_dev):
            place = pl.ds(t * heads + h * group, group)
            if merging:
                outs[0][pl.ds(g * per, per), x ^ job[2], place, :] = value[:, t]
            else:
                outs[job[3]][(*job[4], pl.ds(g * per, per), place, slice(None))] = value[:, t]

    def put_stat(job, g, lines):
        stat = stat_block(lines, dh)
        for i in range(per):
            if merging:
                outs[0][g * per + i, x ^ job[2], tok_dev * heads :, :] = stat
            else:
                outs[job[3]][(*job[4], g * per + i, slice(tok_dev * heads, None), slice(None))] = stat

    def half(job, h, s_ref, lanes_top, later):
        top = jnp.max(lanes_top, axis=1, keepdims=True)
        acc = None
        next_top = None
        if later is not None:
            next_qx, next_h, next_ref = load(*later[:2]), later[1], later[2]
        for span in spans:
            if later is not None:
                next_top = score(next_qx, next_h, next_ref, span, next_top)
            p = jnp.exp2((s_ref[:, span[0] : span[1]] - top) * scale).astype(jnp.bfloat16)
            term = jnp.dot(p, vx_ref[h, span[0] : span[1], :], preferred_element_type=jnp.float32)
            acc = term if acc is None else acc + term
        total_l = acc[:, dh:]
        o = acc[:, :dh] / total_l
        lse = jnp.where(top > 0.5 * NEG, top * scale + jnp.log2(total_l), NEG)
        lines = []
        for g in range(groups):
            mine = lse[g * dh : (g + 1) * dh]
            value = o[g * dh : (g + 1) * dh]
            if merging:
                theirs = column(line_of(got_ref[job[2], g * per, tok_dev * heads :, :], h))
                o_theirs = rows_of(got_ref, (job[2],), g, h, tok_dev, heads, group, dh)
                value, mine = merge_pair(value, mine, o_theirs, theirs)
            put(job, g, h, value)
            lines.append(jnp.sum(jnp.where(diag, mine, 0.0), axis=0, keepdims=True))
        return lines, next_top

    first = load(jobs[0], 0)
    top = None
    for span in spans:
        top = score(first, 0, sa_ref, span, top)
    if merging:
        for g in range(groups):
            lines = []
            for h in range(kv):
                at = (g * per, slice(tok_dev * heads, None), slice(None))
                pair = ((own_ref, ()), (got_ref, (0,)))
                lse = [column(line_of(ref[(*first_at, *at)], h)) for ref, first_at in pair]
                o = [rows_of(ref, first_at, g, h, tok_dev, heads, group, dh) for ref, first_at in pair]
                value, mine = merge_pair(o[0], lse[0], o[1], lse[1])
                put((0, 0, 0), g, h, value)
                mine = jnp.broadcast_to(mine, (dh, dh))
                lines.append(jnp.sum(jnp.where(diag, mine, 0.0), axis=0, keepdims=True))
            put_stat((0, 0, 0), g, lines)
    for i, job in enumerate(jobs):
        lines_a, top = half(job, 0, sa_ref, top, (job, 1, sb_ref))
        later = (jobs[i + 1], 0, sa_ref) if i + 1 < len(jobs) else None
        lines_b, top = half(job, 1, sb_ref, top, later)
        for g in range(groups):
            put_stat(job, g, (lines_a[g], lines_b[g]))


def attend(jobs, queries, feat, kx, vx, out_shapes, merge_with=()):
    count, tok_dev, heads, dh = queries[0].shape
    kv, _, total = kx.shape
    n = count * tok_dev * heads // kv
    work = n * kv * len(jobs) * total
    shapes = [jax.ShapeDtypeStruct(shape, jnp.bfloat16) for shape in out_shapes]
    return pl.pallas_call(
        functools.partial(attend_kernel, jobs, len(queries), bool(merge_with)),
        in_specs=[VMEM] * (len(queries) + 3 + len(merge_with)),
        out_specs=[VMEM] * len(shapes),
        out_shape=shapes,
        scratch_shapes=[
            pltpu.VMEM((n, total), jnp.float32),
            pltpu.VMEM((n, total), jnp.float32),
        ],
        compiler_params=pltpu.CompilerParams(vmem_limit_bytes=26 * 2**20),
        cost_estimate=pl.CostEstimate(flops=8 * work * dh, bytes_accessed=5 * 2**20, transcendentals=work),
    )(*queries, feat, kx, vx, *merge_with)


def replicate_kernel(in_ref, out_ref):
    value = in_ref[...]
    for i in range(out_ref.shape[0]):
        out_ref[i] = value


def replicate(a, count):
    return pl.pallas_call(
        replicate_kernel,
        in_specs=[VMEM],
        out_specs=VMEM,
        out_shape=jax.ShapeDtypeStruct((count,) + a.shape, a.dtype),
    )(a)


def merge_kernel(rows, in_ref, out_ref, flat_ref):
    count, _, dh = in_ref.shape
    kv = 2
    z = lax.axis_index("z")
    lines = []
    for h in range(kv):
        parts = []
        for i in range(count):
            block = in_ref[i, kv * rows :, :].astype(jnp.float32)
            parts.append(block[3 * h : 3 * h + 1] + block[3 * h + 1 : 3 * h + 2] + block[3 * h + 2 : 3 * h + 3])
        lines.append(jnp.concatenate(parts, axis=0))
    for h in range(kv):
        lse = lines[h]
        high = jnp.max(lse, axis=0, keepdims=True)
        w = jnp.exp2(lse - high)
        w = w / jnp.sum(w, axis=0, keepdims=True)
        w = jnp.concatenate([w, jnp.zeros((dh - count, dh), jnp.float32)], axis=0)
        wt = w.T
        mine = jnp.zeros((rows, dh), jnp.float32)
        for i in range(dh // rows):
            mine = jnp.where(z % (dh // rows) == i, wt[i * rows : (i + 1) * rows], mine)
        group = rows // 2
        acc = jnp.zeros((rows, dh), jnp.float32)
        for i in range(count):
            blocks = [in_ref[i, t * 2 * group + h * group : t * 2 * group + (h + 1) * group, :] for t in range(2)]
            acc = acc + mine[:, i : i + 1] * jnp.concatenate(blocks, axis=0).astype(jnp.float32)
        for t in range(2):
            for j in range(group):
                at = (h * group + j) * dh
                flat_ref[t : t + 1, at : at + dh] = acc[t * group + j : t * group + j + 1]
    value = flat_ref[...].astype(jnp.bfloat16)
    for i in range(count):
        out_ref[i] = value


def merge(got, rows):
    count, _, dh = got.shape
    width = 2 * rows // 2 * dh
    return pl.pallas_call(
        functools.partial(merge_kernel, rows),
        out_shape=jax.ShapeDtypeStruct((count, 2, width), jnp.bfloat16),
        in_specs=[pl.BlockSpec(memory_space=pltpu.VMEM)],
        out_specs=pl.BlockSpec(memory_space=pltpu.VMEM),
        scratch_shapes=[pltpu.VMEM((2, width), jnp.float32)],
        compiler_params=pltpu.CompilerParams(vmem_limit_bytes=16 * 2**20),
    )(got)


def body(queries, cache_keys, cache_values, stretch_keys, stretch_values, valid_lens, offsets, seq_lengths, out_weight):
    tok_dev, heads, dh = queries.shape
    kv = cache_keys.shape[1]
    group = heads // kv
    count = lax.axis_size("z") * lax.axis_size("x")
    rows = tok_dev * group
    c = lax.axis_index("c")
    zx = ("z", "x")
    swap = lambda a: lax.ppermute(a, "c", [(0, 1), (1, 0)])
    everywhere = lambda a: lax.all_to_all(a, zx, 0, 0, tiled=True)

    deep, ways = lax.axis_size("z"), lax.axis_size("x")
    tile = deep * rows
    mine = [lax.all_to_all(jnp.broadcast_to(queries[None], (deep,) + queries.shape), "z", 0, 0, tiled=True)]
    keys = cache_keys.transpose(1, 0, 2)
    values = cache_values.transpose(1, 0, 2)
    mine[0], keys, values = lax.optimization_barrier((mine[0], keys, values))
    kx, vx, feat = prepare(offsets, seq_lengths, valid_lens, keys, values, stretch_keys, stretch_values, ways, tile)
    for d in range(1, ways):
        mine.append(lax.ppermute(mine[0], "x", [(i, i ^ d) for i in range(ways)]))
    block = (deep, tok_dev * heads + 8, dh)
    (near,) = attend([(0, 0, 0, 0, ())], mine[:1], feat, kx, vx, [block])
    *late, feat = lax.optimization_barrier((*mine, feat))
    theirs = [swap(q) for q in late]
    jobs = [(d, 1, d, 0, (d,)) for d in range(ways)]
    (away,) = attend(jobs, theirs, feat, kx, vx, [(ways,) + block])
    jobs = [(d - 1, 0, d, 0, ()) for d in range(1, ways)]
    (part,) = attend(jobs, mine[1:], feat, kx, vx, [(deep, ways) + block[1:]], (near, swap(away)))
    part = part.reshape((count,) + block[1:])
    attended = everywhere(merge(everywhere(part), rows))
    attended_other = swap(attended)
    width = attended.shape[-1]
    project = lambda a: jnp.dot(a.reshape(count * tok_dev, width), out_weight, preferred_element_type=jnp.float32)
    near, far = project(attended), project(attended_other)
    ways = lax.axis_size("head")
    cols = out_weight.shape[1]
    terms = jnp.stack([a.reshape(ways, count // ways, tok_dev, cols) for a in (near, far)], axis=1)
    y = lax.axis_index("head")
    piece = lambda d: lax.dynamic_index_in_dim(terms, y ^ d, 0, keepdims=False)
    total = piece(0)
    for d in range(1, ways):
        total = total + lax.ppermute(piece(d), "head", [(i, i ^ d) for i in range(ways)])
    terms = total
    first = jnp.where(c == 0, terms[0], terms[1])
    second = jnp.where(c == 0, terms[1], terms[0])
    return jnp.stack([first, second], axis=1).reshape(-1, cols).astype(jnp.bfloat16)


def solution(mesh):
    grid = Mesh(mesh.devices.reshape(8, 4, 2, 4), ("z", "x", "c", "head"))
    blk = ("z", "x", "c")
    return jax.shard_map(
        body,
        mesh=grid,
        in_specs=(
            P(blk, "head", None),
            P(blk, "head", None),
            P(blk, "head", None),
            P(blk, "head", None),
            P(blk, "head", None),
            P(blk),
            P(),
            P(),
            P("head", blk),
        ),
        out_specs=P("head", blk),
        check_vma=False,
    )
```

```python
import functools

import jax
import jax.numpy as jnp
from jax import lax
from jax.experimental import pallas as pl
from jax.experimental.pallas import tpu as pltpu
from jax.sharding import Mesh, PartitionSpec as P

NEG = -1e30
LOG2E = 1.4426950408889634


def split3(x):
    hi = x.astype(jnp.bfloat16).astype(jnp.float32)
    rest = x - hi
    mid = rest.astype(jnp.bfloat16).astype(jnp.float32)
    low = (rest - mid).astype(jnp.bfloat16).astype(jnp.float32)
    return hi, mid, low


def seq_of(token, lens_ref, nseq):
    end = jnp.int32(0)
    which = jnp.zeros(token.shape, jnp.int32)
    for i in range(nseq):
        end = end + lens_ref[i]
        which = which + (token >= end).astype(jnp.int32)
    return which


def prepare_kernel(nseq, bounds_ref, lens_ref, k_ref, v_ref, sk_ref, sv_ref, kx_ref, vx_ref, feat_ref):
    kv, cache_dev, dh = k_ref.shape
    total = vx_ref.shape[1]
    tok_dev = sk_ref.shape[0]
    z, x, c = lax.axis_index("z"), lax.axis_index("x"), lax.axis_index("c")
    me = (z * lax.axis_size("x") + x) * 2 + c
    pos = lax.broadcasted_iota(jnp.int32, (dh, cache_dev), 1)
    row = lax.broadcasted_iota(jnp.int32, (dh, 1), 0)
    thr = jnp.full((dh, 1), total, jnp.int32)
    for i in range(nseq):
        thr = jnp.where(row == i, bounds_ref[i], thr)
    bias = jnp.where(pos >= thr, NEG, 0.0).astype(jnp.bfloat16)
    tail_pos = lax.broadcasted_iota(jnp.int32, (dh, dh), 1)
    tail_row = lax.broadcasted_iota(jnp.int32, (dh, dh), 0)
    tail = jnp.where((tail_pos >= tok_dev) & (tail_row < nseq), NEG, 0.0)
    tail = jnp.where((tail_pos < tok_dev) & (tail_row == nseq + tail_pos), 1.0, tail).astype(jnp.bfloat16)
    pad = jnp.zeros((dh - tok_dev, dh), jnp.float32)
    sk = sk_ref[...].astype(jnp.float32)
    sv = sv_ref[...].astype(jnp.float32)
    for h in range(kv):
        kx_ref[h, :dh, :cache_dev] = k_ref[h].T
        kx_ref[h, :dh, cache_dev:] = jnp.concatenate([sk[:, h], pad], axis=0).T.astype(jnp.bfloat16)
        kx_ref[h, dh:, :cache_dev] = bias
        kx_ref[h, dh:, cache_dev:] = tail
        vx_ref[h, :cache_dev, :dh] = v_ref[h]
        vx_ref[h, cache_dev:, :dh] = jnp.concatenate([sv[:, h], pad], axis=0).astype(jnp.bfloat16)
        vx_ref[h, :, dh:] = jnp.ones((total, dh), jnp.bfloat16)
    sides, ways, tile, _ = feat_ref.shape
    toks = tile // GROUP
    r = lax.broadcasted_iota(jnp.int32, (toks, dh), 0)
    lane = lax.broadcasted_iota(jnp.int32, (toks, dh), 1)
    for side in range(sides):
        core = c if side == 0 else 1 - c
        for d in range(ways):
            place = r // tok_dev * ways + (x ^ d)
            token = (place * 2 + core) * tok_dev + r % tok_dev
            seq = seq_of(token, lens_ref, nseq)
            feat = (lane == seq).astype(jnp.float32)
            for i in range(tok_dev):
                u = me * tok_dev + i
                useq = jnp.int32(0)
                end = jnp.int32(0)
                for n in range(nseq):
                    end = end + lens_ref[n]
                    useq = useq + (u >= end).astype(jnp.int32)
                seen = (seq == useq) & (u <= token)
                feat = jnp.where((lane == nseq + i) & jnp.logical_not(seen), NEG, feat)
            feat = jnp.broadcast_to(feat[:, None, :], (toks, GROUP, dh)).reshape(tile, dh)
            feat_ref[side, d] = feat.astype(jnp.bfloat16)


GROUP = 16
VMEM = pl.BlockSpec(memory_space=pltpu.VMEM)
SMEM = pl.BlockSpec(memory_space=pltpu.SMEM)


def prepare(bounds, lens, k, v, sk, sv, ways, tile):
    kv, cache_dev, dh = k.shape
    total = cache_dev + dh
    keys = jax.ShapeDtypeStruct((kv, 2 * dh, total), jnp.bfloat16)
    values = jax.ShapeDtypeStruct((kv, total, 2 * dh), jnp.bfloat16)
    return pl.pallas_call(
        functools.partial(prepare_kernel, bounds.shape[0]),
        in_specs=[SMEM] * 2 + [VMEM] * 4,
        out_specs=[VMEM] * 3,
        out_shape=[keys, values, jax.ShapeDtypeStruct((2, ways, tile, dh), jnp.bfloat16)],
        compiler_params=pltpu.CompilerParams(vmem_limit_bytes=16 * 2**20),
        cost_estimate=pl.CostEstimate(flops=2 * kv * total * dh * 8, bytes_accessed=8 * 2**20, transcendentals=0),
    )(bounds, lens, k, v, sk, sv)


def stat_block(lines, dh):
    sub = lax.broadcasted_iota(jnp.int32, (8, dh), 0)
    stat = jnp.zeros((8, dh), jnp.float32)
    for h, line in enumerate(lines):
        for i, part in enumerate(split3(line)):
            stat = jnp.where(sub == 3 * h + i, part, stat)
    return stat.astype(jnp.bfloat16)


def line_of(block, h):
    block = block.astype(jnp.float32)
    return block[3 * h : 3 * h + 1] + block[3 * h + 1 : 3 * h + 2] + block[3 * h + 2 : 3 * h + 3]


def rows_of(ref, at, g, h, tok_dev, heads, group, dh):
    per = dh // (tok_dev * group)
    where = pl.ds(g * per, per)
    parts = [ref[(*at, where, pl.ds(t * heads + h * group, group), slice(None))] for t in range(tok_dev)]
    return jnp.stack(parts, axis=1).reshape(dh, dh).astype(jnp.float32)


def attend_kernel(jobs, n_q, plain, merging, *refs):
    q_refs = refs[:n_q]
    feat_ref, kx_ref, vx_ref = refs[n_q : n_q + 3]
    rest = refs[n_q + 3 :]
    if merging:
        own_refs, (got_ref, out_ref) = rest[:plain], rest[plain : plain + 2]
        outs, rest = [out_ref], rest[plain + 2 :]
    else:
        n_out = 1 + max(job[3] for job in jobs)
        outs, rest = list(rest[:n_out]), rest[n_out:]
    sa_ref, sb_ref = rest
    count, tok_dev, heads, dh = q_refs[0].shape
    kv, _, total = kx_ref.shape
    group = heads // kv
    n = count * tok_dev * group
    per = dh // (tok_dev * group)
    groups = n // dh
    scale = LOG2E * dh ** (-0.5)
    edges = [0, 512, 1024, 1536, total]
    spans = list(zip(edges[:-1], edges[1:]))
    diag = lax.broadcasted_iota(jnp.int32, (dh, dh), 0) == lax.broadcasted_iota(jnp.int32, (dh, dh), 1)
    x = lax.axis_index("x")

    def load(job, h):
        q = q_refs[job[0]][:, :, h * group : (h + 1) * group, :].reshape(n, dh)
        return jnp.concatenate([q, feat_ref[job[1], job[2]]], axis=1)

    def score(qx, h, s_ref, span, top):
        s = jnp.dot(qx, kx_ref[h, :, span[0] : span[1]], preferred_element_type=jnp.float32)
        s_ref[:, span[0] : span[1]] = s
        for i in range((span[1] - span[0]) // dh):
            part = s[:, i * dh : (i + 1) * dh]
            top = part if top is None else jnp.maximum(top, part)
        return top

    def merge_pair(value, mine, o_theirs, theirs):
        high = jnp.maximum(mine, theirs)
        a, b = jnp.exp2(mine - high), jnp.exp2(theirs - high)
        both = a + b
        return (value * a + o_theirs * b) / both, high + jnp.log2(both)

    def column(line):
        return jnp.sum(jnp.where(diag, line, 0.0), axis=1, keepdims=True)

    def put(job, g, h, value):
        value = value.reshape(per, tok_dev, group, dh).astype(jnp.bfloat16)
        for t in range(tok_dev):
            place = pl.ds(t * heads + h * group, group)
            if merging:
                outs[0][pl.ds(g * per, per), x ^ job[2], place, :] = value[:, t]
            else:
                outs[job[3]][(*job[4], pl.ds(g * per, per), place, slice(None))] = value[:, t]

    def put_stat(job, g, lines):
        stat = stat_block(lines, dh)
        for i in range(per):
            if merging:
                outs[0][g * per + i, x ^ job[2], tok_dev * heads :, :] = stat
            else:
                outs[job[3]][(*job[4], g * per + i, slice(tok_dev * heads, None), slice(None))] = stat

    def half(job, h, s_ref, lanes_top, later):
        top = jnp.max(lanes_top, axis=1, keepdims=True)
        acc = None
        next_top = None
        if later is not None:
            next_qx, next_h, next_ref = load(*later[:2]), later[1], later[2]
        for span in spans:
            if later is not None:
                next_top = score(next_qx, next_h, next_ref, span, next_top)
            p = jnp.exp2((s_ref[:, span[0] : span[1]] - top) * scale).astype(jnp.bfloat16)
            term = jnp.dot(p, vx_ref[h, span[0] : span[1], :], preferred_element_type=jnp.float32)
            acc = term if acc is None else acc + term
        total_l = acc[:, dh:]
        o = acc[:, :dh] / total_l
        lse = jnp.where(top > 0.5 * NEG, top * scale + jnp.log2(total_l), NEG)
        lines = []
        for g in range(groups):
            mine = lse[g * dh : (g + 1) * dh]
            value = o[g * dh : (g + 1) * dh]
            if merging:
                theirs = column(line_of(got_ref[job[2], g * per, tok_dev * heads :, :], h))
                o_theirs = rows_of(got_ref, (job[2],), g, h, tok_dev, heads, group, dh)
                value, mine = merge_pair(value, mine, o_theirs, theirs)
            put(job, g, h, value)
            lines.append(jnp.sum(jnp.where(diag, mine, 0.0), axis=0, keepdims=True))
        return lines, next_top

    first = load(jobs[0], 0)
    top = None
    for span in spans:
        top = score(first, 0, sa_ref, span, top)
    if merging:
        for d in range(plain):
            for g in range(groups):
                lines = []
                for h in range(kv):
                    at = (g * per, slice(tok_dev * heads, None), slice(None))
                    pair = ((own_refs[d], ()), (got_ref, (d,)))
                    lse = [column(line_of(ref[(*first_at, *at)], h)) for ref, first_at in pair]
                    o = [rows_of(ref, first_at, g, h, tok_dev, heads, group, dh) for ref, first_at in pair]
                    value, mine = merge_pair(o[0], lse[0], o[1], lse[1])
                    put((0, 0, d), g, h, value)
                    mine = jnp.broadcast_to(mine, (dh, dh))
                    lines.append(jnp.sum(jnp.where(diag, mine, 0.0), axis=0, keepdims=True))
                put_stat((0, 0, d), g, lines)
    for i, job in enumerate(jobs):
        lines_a, top = half(job, 0, sa_ref, top, (job, 1, sb_ref))
        later = (jobs[i + 1], 0, sa_ref) if i + 1 < len(jobs) else None
        lines_b, top = half(job, 1, sb_ref, top, later)
        for g in range(groups):
            put_stat(job, g, (lines_a[g], lines_b[g]))


def attend(jobs, queries, feat, kx, vx, out_shapes, merge_with=()):
    count, tok_dev, heads, dh = queries[0].shape
    kv, _, total = kx.shape
    n = count * tok_dev * heads // kv
    work = n * kv * len(jobs) * total
    shapes = [jax.ShapeDtypeStruct(shape, jnp.bfloat16) for shape in out_shapes]
    return pl.pallas_call(
        functools.partial(attend_kernel, jobs, len(queries), max(len(merge_with) - 1, 0), bool(merge_with)),
        in_specs=[VMEM] * (len(queries) + 3 + len(merge_with)),
        out_specs=[VMEM] * len(shapes),
        out_shape=shapes,
        scratch_shapes=[
            pltpu.VMEM((n, total), jnp.float32),
            pltpu.VMEM((n, total), jnp.float32),
        ],
        compiler_params=pltpu.CompilerParams(vmem_limit_bytes=26 * 2**20),
        cost_estimate=pl.CostEstimate(flops=8 * work * dh, bytes_accessed=5 * 2**20, transcendentals=work),
    )(*queries, feat, kx, vx, *merge_with)


def merge_kernel(rows, in_ref, out_ref, flat_ref):
    count, _, dh = in_ref.shape
    kv = 2
    z = lax.axis_index("z")
    lines = []
    for h in range(kv):
        parts = []
        for i in range(count):
            block = in_ref[i, kv * rows :, :].astype(jnp.float32)
            parts.append(block[3 * h : 3 * h + 1] + block[3 * h + 1 : 3 * h + 2] + block[3 * h + 2 : 3 * h + 3])
        lines.append(jnp.concatenate(parts, axis=0))
    for h in range(kv):
        lse = lines[h]
        high = jnp.max(lse, axis=0, keepdims=True)
        w = jnp.exp2(lse - high)
        w = w / jnp.sum(w, axis=0, keepdims=True)
        w = jnp.concatenate([w, jnp.zeros((dh - count, dh), jnp.float32)], axis=0)
        wt = w.T
        mine = jnp.zeros((rows, dh), jnp.float32)
        for i in range(dh // rows):
            mine = jnp.where(z % (dh // rows) == i, wt[i * rows : (i + 1) * rows], mine)
        group = rows // 2
        acc = jnp.zeros((rows, dh), jnp.float32)
        for i in range(count):
            blocks = [in_ref[i, t * 2 * group + h * group : t * 2 * group + (h + 1) * group, :] for t in range(2)]
            acc = acc + mine[:, i : i + 1] * jnp.concatenate(blocks, axis=0).astype(jnp.float32)
        for t in range(2):
            for j in range(group):
                at = (h * group + j) * dh
                flat_ref[t : t + 1, at : at + dh] = acc[t * group + j : t * group + j + 1]
    value = flat_ref[...].astype(jnp.bfloat16)
    for i in range(count):
        out_ref[i] = value


def merge(got, rows):
    count, _, dh = got.shape
    width = 2 * rows // 2 * dh
    return pl.pallas_call(
        functools.partial(merge_kernel, rows),
        out_shape=jax.ShapeDtypeStruct((count, 2, width), jnp.bfloat16),
        in_specs=[pl.BlockSpec(memory_space=pltpu.VMEM)],
        out_specs=pl.BlockSpec(memory_space=pltpu.VMEM),
        scratch_shapes=[pltpu.VMEM((2, width), jnp.float32)],
        compiler_params=pltpu.CompilerParams(vmem_limit_bytes=16 * 2**20),
    )(got)


def body(queries, cache_keys, cache_values, stretch_keys, stretch_values, valid_lens, offsets, seq_lengths, out_weight):
    tok_dev, heads, dh = queries.shape
    kv = cache_keys.shape[1]
    group = heads // kv
    count = lax.axis_size("z") * lax.axis_size("x")
    rows = tok_dev * group
    c = lax.axis_index("c")
    zx = ("z", "x")
    swap = lambda a: lax.ppermute(a, "c", [(0, 1), (1, 0)])
    everywhere = lambda a: lax.all_to_all(a, zx, 0, 0, tiled=True)

    deep, ways = lax.axis_size("z"), lax.axis_size("x")
    tile = deep * rows
    mine = [lax.all_to_all(jnp.broadcast_to(queries[None], (deep,) + queries.shape), "z", 0, 0, tiled=True)]
    keys = cache_keys.transpose(1, 0, 2)
    values = cache_values.transpose(1, 0, 2)
    me = (lax.axis_index("z") * ways + lax.axis_index("x")) * 2 + c
    bounds = jnp.minimum(valid_lens, offsets - me * cache_keys.shape[0])
    mine[0], keys, values, bounds = lax.optimization_barrier((mine[0], keys, values, bounds))
    kx, vx, feat = prepare(bounds, seq_lengths, keys, values, stretch_keys, stretch_values, ways, tile)
    for d in range(1, ways):
        mine.append(lax.ppermute(mine[0], "x", [(i, i ^ d) for i in range(ways)]))
    block = (deep, tok_dev * heads + 8, dh)
    near = [attend([(0, 0, d, 0, ())], [mine[d]], feat, kx, vx, [block])[0] for d in range(3)]
    *late, near[0] = lax.optimization_barrier((*mine, near[0]))
    theirs = [swap(q) for q in late]
    *theirs, near[1] = lax.optimization_barrier((*theirs, near[1]))
    jobs = [(d, 1, d, 0, (d,)) for d in range(ways)]
    (away,) = attend(jobs, theirs, feat, kx, vx, [(ways,) + block])
    rest = range(len(near), ways)
    jobs = [(i, 0, d, 0, ()) for i, d in enumerate(rest)]
    merge_with = (*near, swap(away))
    (part,) = attend(jobs, [mine[d] for d in rest], feat, kx, vx, [(deep, ways) + block[1:]], merge_with)
    part = part.reshape((count,) + block[1:])
    attended = everywhere(merge(everywhere(part), rows))
    attended_other = swap(attended)
    width = attended.shape[-1]
    project = lambda a: jnp.dot(a.reshape(count * tok_dev, width), out_weight, preferred_element_type=jnp.float32)
    near, far = project(attended), project(attended_other)
    ways = lax.axis_size("head")
    cols = out_weight.shape[1]
    terms = jnp.stack([a.reshape(ways, count // ways, tok_dev, cols) for a in (near, far)], axis=1)
    y = lax.axis_index("head")
    piece = lambda d: lax.dynamic_index_in_dim(terms, y ^ d, 0, keepdims=False)
    total = piece(0)
    for d in range(1, ways):
        total = total + lax.ppermute(piece(d), "head", [(i, i ^ d) for i in range(ways)])
    terms = total
    first = jnp.where(c == 0, terms[0], terms[1])
    second = jnp.where(c == 0, terms[1], terms[0])
    return jnp.stack([first, second], axis=1).reshape(-1, cols).astype(jnp.bfloat16)


def solution(mesh):
    grid = Mesh(mesh.devices.reshape(8, 4, 2, 4), ("z", "x", "c", "head"))
    blk = ("z", "x", "c")
    return jax.shard_map(
        body,
        mesh=grid,
        in_specs=(
            P(blk, "head", None),
            P(blk, "head", None),
            P(blk, "head", None),
            P(blk, "head", None),
            P(blk, "head", None),
            P(blk),
            P(),
            P(),
            P("head", blk),
        ),
        out_specs=P("head", blk),
        check_vma=False,
    )
```

```python
import functools

import jax
import jax.numpy as jnp
from jax import lax
from jax.experimental import pallas as pl
from jax.experimental.pallas import tpu as pltpu
from jax.sharding import Mesh, PartitionSpec as P

NEG = -1e30
LOG2E = 1.4426950408889634


def split3(x):
    hi = x.astype(jnp.bfloat16).astype(jnp.float32)
    rest = x - hi
    mid = rest.astype(jnp.bfloat16).astype(jnp.float32)
    low = (rest - mid).astype(jnp.bfloat16).astype(jnp.float32)
    return hi, mid, low


def seq_of(token, lens_ref, nseq):
    end = jnp.int32(0)
    which = jnp.zeros(token.shape, jnp.int32)
    for i in range(nseq):
        end = end + lens_ref[i]
        which = which + (token >= end).astype(jnp.int32)
    return which


def prepare_kernel(nseq, bounds_ref, lens_ref, k_ref, v_ref, sk_ref, sv_ref, kx_ref, vx_ref, feat_ref):
    kv, cache_dev, dh = k_ref.shape
    total = vx_ref.shape[1]
    tok_dev = sk_ref.shape[0]
    z, x, c = lax.axis_index("z"), lax.axis_index("x"), lax.axis_index("c")
    me = (z * lax.axis_size("x") + x) * 2 + c
    pos = lax.broadcasted_iota(jnp.int32, (dh, cache_dev), 1)
    row = lax.broadcasted_iota(jnp.int32, (dh, 1), 0)
    thr = jnp.full((dh, 1), total, jnp.int32)
    for i in range(nseq):
        thr = jnp.where(row == i, bounds_ref[i], thr)
    bias = jnp.where(pos >= thr, NEG, 0.0).astype(jnp.bfloat16)
    tail_pos = lax.broadcasted_iota(jnp.int32, (dh, dh), 1)
    tail_row = lax.broadcasted_iota(jnp.int32, (dh, dh), 0)
    tail = jnp.where((tail_pos >= tok_dev) & (tail_row < nseq), NEG, 0.0)
    tail = jnp.where((tail_pos < tok_dev) & (tail_row == nseq + tail_pos), 1.0, tail).astype(jnp.bfloat16)
    pad = jnp.zeros((dh - tok_dev, dh), jnp.float32)
    sk = sk_ref[...].astype(jnp.float32)
    sv = sv_ref[...].astype(jnp.float32)
    for h in range(kv):
        kx_ref[h, :dh, :cache_dev] = k_ref[h].T
        kx_ref[h, :dh, cache_dev:] = jnp.concatenate([sk[:, h], pad], axis=0).T.astype(jnp.bfloat16)
        kx_ref[h, dh:, :cache_dev] = bias
        kx_ref[h, dh:, cache_dev:] = tail
        vx_ref[h, :cache_dev, :dh] = v_ref[h]
        vx_ref[h, cache_dev:, :dh] = jnp.concatenate([sv[:, h], pad], axis=0).astype(jnp.bfloat16)
        vx_ref[h, :, dh:] = jnp.ones((total, dh), jnp.bfloat16)
    sides, ways, tile, _ = feat_ref.shape
    toks = tile // GROUP
    r = lax.broadcasted_iota(jnp.int32, (toks, dh), 0)
    lane = lax.broadcasted_iota(jnp.int32, (toks, dh), 1)
    for side in range(sides):
        core = c if side == 0 else 1 - c
        for d in range(ways):
            place = r // tok_dev * ways + (x ^ d)
            token = (place * 2 + core) * tok_dev + r % tok_dev
            seq = seq_of(token, lens_ref, nseq)
            feat = (lane == seq).astype(jnp.float32)
            for i in range(tok_dev):
                u = me * tok_dev + i
                useq = jnp.int32(0)
                end = jnp.int32(0)
                for n in range(nseq):
                    end = end + lens_ref[n]
                    useq = useq + (u >= end).astype(jnp.int32)
                seen = (seq == useq) & (u <= token)
                feat = jnp.where((lane == nseq + i) & jnp.logical_not(seen), NEG, feat)
            feat = jnp.broadcast_to(feat[:, None, :], (toks, GROUP, dh)).reshape(tile, dh)
            feat_ref[side, d] = feat.astype(jnp.bfloat16)


GROUP = 16
VMEM = pl.BlockSpec(memory_space=pltpu.VMEM)
SMEM = pl.BlockSpec(memory_space=pltpu.SMEM)


def prepare(bounds, lens, k, v, sk, sv, ways, tile):
    kv, cache_dev, dh = k.shape
    total = cache_dev + dh
    keys = jax.ShapeDtypeStruct((kv, 2 * dh, total), jnp.bfloat16)
    values = jax.ShapeDtypeStruct((kv, total, 2 * dh), jnp.bfloat16)
    return pl.pallas_call(
        functools.partial(prepare_kernel, bounds.shape[0]),
        in_specs=[SMEM] * 2 + [VMEM] * 4,
        out_specs=[VMEM] * 3,
        out_shape=[keys, values, jax.ShapeDtypeStruct((2, ways, tile, dh), jnp.bfloat16)],
        compiler_params=pltpu.CompilerParams(vmem_limit_bytes=16 * 2**20),
        cost_estimate=pl.CostEstimate(flops=2 * kv * total * dh * 8, bytes_accessed=8 * 2**20, transcendentals=0),
    )(bounds, lens, k, v, sk, sv)


def stat_block(lines, dh):
    sub = lax.broadcasted_iota(jnp.int32, (8, dh), 0)
    stat = jnp.zeros((8, dh), jnp.float32)
    for h, line in enumerate(lines):
        for i, part in enumerate(split3(line)):
            stat = jnp.where(sub == 3 * h + i, part, stat)
    return stat.astype(jnp.bfloat16)


def line_of(block, h):
    block = block.astype(jnp.float32)
    return block[3 * h : 3 * h + 1] + block[3 * h + 1 : 3 * h + 2] + block[3 * h + 2 : 3 * h + 3]


def rows_of(ref, at, g, h, tok_dev, heads, group, dh):
    per = dh // (tok_dev * group)
    where = pl.ds(g * per, per)
    parts = [ref[(*at, where, pl.ds(t * heads + h * group, group), slice(None))] for t in range(tok_dev)]
    return jnp.stack(parts, axis=1).reshape(dh, dh).astype(jnp.float32)


def attend_kernel(jobs, n_q, plain, merging, *refs):
    q_refs = refs[:n_q]
    feat_ref, kx_ref, vx_ref = refs[n_q : n_q + 3]
    rest = refs[n_q + 3 :]
    if merging:
        own_refs, (got_ref, out_ref) = rest[:plain], rest[plain : plain + 2]
        outs, rest = [out_ref], rest[plain + 2 :]
    else:
        n_out = 1 + max(part[3] for job in jobs for part in job)
        outs, rest = list(rest[:n_out]), rest[n_out:]
    sa_ref, sb_ref = rest
    count, tok_dev, heads, dh = q_refs[0].shape
    kv, _, total = kx_ref.shape
    group = heads // kv
    n = count * tok_dev * group
    per = dh // (tok_dev * group)
    groups = n // dh
    scale = LOG2E * dh ** (-0.5)
    edges = [0, 512, 1024, 1536, total]
    spans = list(zip(edges[:-1], edges[1:]))
    diag = lax.broadcasted_iota(jnp.int32, (dh, dh), 0) == lax.broadcasted_iota(jnp.int32, (dh, dh), 1)
    x = lax.axis_index("x")

    def load(job, h):
        q = [q_refs[part[0]][:, :, h * group : (h + 1) * group, :].reshape(n, dh) for part in job]
        feat = [feat_ref[part[1], part[2]] for part in job]
        rows = [jnp.concatenate(pair, axis=1) for pair in zip(q, feat)]
        return rows[0] if len(rows) == 1 else jnp.concatenate(rows, axis=0)

    def score(qx, h, s_ref, span, top):
        s = jnp.dot(qx, kx_ref[h, :, span[0] : span[1]], preferred_element_type=jnp.float32)
        s_ref[:, span[0] : span[1]] = s
        for i in range((span[1] - span[0]) // dh):
            part = s[:, i * dh : (i + 1) * dh]
            top = part if top is None else jnp.maximum(top, part)
        return top

    def merge_pair(value, mine, o_theirs, theirs):
        high = jnp.maximum(mine, theirs)
        a, b = jnp.exp2(mine - high), jnp.exp2(theirs - high)
        both = a + b
        return (value * a + o_theirs * b) / both, high + jnp.log2(both)

    def column(line):
        return jnp.sum(jnp.where(diag, line, 0.0), axis=1, keepdims=True)

    def put(job, g, h, value):
        value = value.reshape(per, tok_dev, group, dh).astype(jnp.bfloat16)
        for t in range(tok_dev):
            place = pl.ds(t * heads + h * group, group)
            if merging:
                outs[0][pl.ds(g * per, per), x ^ job[2], place, :] = value[:, t]
            else:
                outs[job[3]][(*job[4], pl.ds(g * per, per), place, slice(None))] = value[:, t]

    def put_stat(job, g, lines):
        stat = stat_block(lines, dh)
        for i in range(per):
            if merging:
                outs[0][g * per + i, x ^ job[2], tok_dev * heads :, :] = stat
            else:
                outs[job[3]][(*job[4], g * per + i, slice(tok_dev * heads, None), slice(None))] = stat

    def half(job, h, s_ref, lanes_top, later):
        top = jnp.max(lanes_top, axis=1, keepdims=True)
        acc = None
        next_top = None
        if later is not None:
            next_qx, next_h, next_ref = load(*later[:2]), later[1], later[2]
        for span in spans:
            if later is not None:
                next_top = score(next_qx, next_h, next_ref, span, next_top)
            p = jnp.exp2((s_ref[:, span[0] : span[1]] - top) * scale).astype(jnp.bfloat16)
            term = jnp.dot(p, vx_ref[h, span[0] : span[1], :], preferred_element_type=jnp.float32)
            acc = term if acc is None else acc + term
        total_l = acc[:, dh:]
        o = acc[:, :dh] / total_l
        lse = jnp.where(top > 0.5 * NEG, top * scale + jnp.log2(total_l), NEG)
        lines = []
        for at in range(groups * len(job)):
            part, g = job[at // groups], at % groups
            mine = lse[at * dh : (at + 1) * dh]
            value = o[at * dh : (at + 1) * dh]
            if merging:
                theirs = column(line_of(got_ref[part[2], g * per, tok_dev * heads :, :], h))
                o_theirs = rows_of(got_ref, (part[2],), g, h, tok_dev, heads, group, dh)
                value, mine = merge_pair(value, mine, o_theirs, theirs)
            put(part, g, h, value)
            lines.append(jnp.sum(jnp.where(diag, mine, 0.0), axis=0, keepdims=True))
        return lines, next_top

    first = load(jobs[0], 0)
    top = None
    for span in spans:
        top = score(first, 0, sa_ref, span, top)
    if merging:
        for d in range(plain):
            for g in range(groups):
                lines = []
                for h in range(kv):
                    at = (g * per, slice(tok_dev * heads, None), slice(None))
                    pair = ((own_refs[d], ()), (got_ref, (d,)))
                    lse = [column(line_of(ref[(*first_at, *at)], h)) for ref, first_at in pair]
                    o = [rows_of(ref, first_at, g, h, tok_dev, heads, group, dh) for ref, first_at in pair]
                    value, mine = merge_pair(o[0], lse[0], o[1], lse[1])
                    put((0, 0, d), g, h, value)
                    mine = jnp.broadcast_to(mine, (dh, dh))
                    lines.append(jnp.sum(jnp.where(diag, mine, 0.0), axis=0, keepdims=True))
                put_stat((0, 0, d), g, lines)
    for i, job in enumerate(jobs):
        lines_a, top = half(job, 0, sa_ref, top, (job, 1, sb_ref))
        later = (jobs[i + 1], 0, sa_ref) if i + 1 < len(jobs) else None
        lines_b, top = half(job, 1, sb_ref, top, later)
        for at in range(groups * len(job)):
            put_stat(job[at // groups], at % groups, (lines_a[at], lines_b[at]))


def attend(jobs, queries, feat, kx, vx, out_shapes, merge_with=()):
    count, tok_dev, heads, dh = queries[0].shape
    kv, _, total = kx.shape
    n = count * tok_dev * heads // kv * max(len(job) for job in jobs)
    work = n * kv * len(jobs) * total
    shapes = [jax.ShapeDtypeStruct(shape, jnp.bfloat16) for shape in out_shapes]
    return pl.pallas_call(
        functools.partial(attend_kernel, jobs, len(queries), max(len(merge_with) - 1, 0), bool(merge_with)),
        in_specs=[VMEM] * (len(queries) + 3 + len(merge_with)),
        out_specs=[VMEM] * len(shapes),
        out_shape=shapes,
        scratch_shapes=[
            pltpu.VMEM((n, total), jnp.float32),
            pltpu.VMEM((n, total), jnp.float32),
        ],
        compiler_params=pltpu.CompilerParams(vmem_limit_bytes=26 * 2**20),
        cost_estimate=pl.CostEstimate(flops=8 * work * dh, bytes_accessed=5 * 2**20, transcendentals=work),
    )(*queries, feat, kx, vx, *merge_with)


def merge_kernel(rows, in_ref, out_ref, flat_ref):
    count, _, dh = in_ref.shape
    kv = 2
    z = lax.axis_index("z")
    lines = []
    for h in range(kv):
        parts = []
        for i in range(count):
            block = in_ref[i, kv * rows :, :].astype(jnp.float32)
            parts.append(block[3 * h : 3 * h + 1] + block[3 * h + 1 : 3 * h + 2] + block[3 * h + 2 : 3 * h + 3])
        lines.append(jnp.concatenate(parts, axis=0))
    for h in range(kv):
        lse = lines[h]
        high = jnp.max(lse, axis=0, keepdims=True)
        w = jnp.exp2(lse - high)
        w = w / jnp.sum(w, axis=0, keepdims=True)
        w = jnp.concatenate([w, jnp.zeros((dh - count, dh), jnp.float32)], axis=0)
        wt = w.T
        mine = jnp.zeros((rows, dh), jnp.float32)
        for i in range(dh // rows):
            mine = jnp.where(z % (dh // rows) == i, wt[i * rows : (i + 1) * rows], mine)
        group = rows // 2
        acc = jnp.zeros((rows, dh), jnp.float32)
        for i in range(count):
            blocks = [in_ref[i, t * 2 * group + h * group : t * 2 * group + (h + 1) * group, :] for t in range(2)]
            acc = acc + mine[:, i : i + 1] * jnp.concatenate(blocks, axis=0).astype(jnp.float32)
        for t in range(2):
            for j in range(group):
                at = (h * group + j) * dh
                flat_ref[t : t + 1, at : at + dh] = acc[t * group + j : t * group + j + 1]
    value = flat_ref[...].astype(jnp.bfloat16)
    for i in range(count):
        out_ref[i] = value


def merge(got, rows):
    count, _, dh = got.shape
    width = 2 * rows // 2 * dh
    return pl.pallas_call(
        functools.partial(merge_kernel, rows),
        out_shape=jax.ShapeDtypeStruct((count, 2, width), jnp.bfloat16),
        in_specs=[pl.BlockSpec(memory_space=pltpu.VMEM)],
        out_specs=pl.BlockSpec(memory_space=pltpu.VMEM),
        scratch_shapes=[pltpu.VMEM((2, width), jnp.float32)],
        compiler_params=pltpu.CompilerParams(vmem_limit_bytes=16 * 2**20),
    )(got)


def body(queries, cache_keys, cache_values, stretch_keys, stretch_values, valid_lens, offsets, seq_lengths, out_weight):
    tok_dev, heads, dh = queries.shape
    kv = cache_keys.shape[1]
    group = heads // kv
    count = lax.axis_size("z") * lax.axis_size("x")
    rows = tok_dev * group
    c = lax.axis_index("c")
    zx = ("z", "x")
    swap = lambda a: lax.ppermute(a, "c", [(0, 1), (1, 0)])
    everywhere = lambda a: lax.all_to_all(a, zx, 0, 0, tiled=True)

    deep, ways = lax.axis_size("z"), lax.axis_size("x")
    tile = deep * rows
    mine = [lax.all_to_all(jnp.broadcast_to(queries[None], (deep,) + queries.shape), "z", 0, 0, tiled=True)]
    values = cache_values.transpose(1, 0, 2)
    me = (lax.axis_index("z") * ways + lax.axis_index("x")) * 2 + c
    bounds = jnp.minimum(valid_lens, offsets - me * cache_keys.shape[0])
    mine[0], cache_keys, values, bounds = lax.optimization_barrier((mine[0], cache_keys, values, bounds))
    keys = cache_keys.transpose(1, 0, 2)
    kx, vx, feat = prepare(bounds, seq_lengths, keys, values, stretch_keys, stretch_values, ways, tile)
    for d in range(1, ways):
        mine.append(lax.ppermute(mine[0], "x", [(i, i ^ d) for i in range(ways)]))
    block = (deep, tok_dev * heads + 8, dh)
    near = [attend([((0, 0, d, 0, ()),)], [mine[d]], feat, kx, vx, [block])[0] for d in range(3)]
    *late, near[0] = lax.optimization_barrier((*mine, near[0]))
    theirs = [swap(q) for q in late]
    *theirs, near[1] = lax.optimization_barrier((*theirs, near[1]))
    jobs = [tuple((d, 1, d, 0, (d,)) for d in pair) for pair in ((0, 1), (2, 3))]
    (away,) = attend(jobs, theirs, feat, kx, vx, [(ways,) + block])
    rest = range(len(near), ways)
    jobs = [((i, 0, d, 0, ()),) for i, d in enumerate(rest)]
    merge_with = (*near, swap(away))
    (part,) = attend(jobs, [mine[d] for d in rest], feat, kx, vx, [(deep, ways) + block[1:]], merge_with)
    part = part.reshape((count,) + block[1:])
    attended = everywhere(merge(everywhere(part), rows))
    attended_other = swap(attended)
    width = attended.shape[-1]
    project = lambda a: jnp.dot(a.reshape(count * tok_dev, width), out_weight, preferred_element_type=jnp.float32)
    near, far = project(attended), project(attended_other)
    ways = lax.axis_size("head")
    cols = out_weight.shape[1]
    terms = jnp.stack([a.reshape(ways, count // ways, tok_dev, cols) for a in (near, far)], axis=1)
    y = lax.axis_index("head")
    piece = lambda d: lax.dynamic_index_in_dim(terms, y ^ d, 0, keepdims=False)
    total = piece(0)
    for d in range(1, ways):
        total = total + lax.ppermute(piece(d), "head", [(i, i ^ d) for i in range(ways)])
    terms = total
    first = jnp.where(c == 0, terms[0], terms[1])
    second = jnp.where(c == 0, terms[1], terms[0])
    return jnp.stack([first, second], axis=1).reshape(-1, cols).astype(jnp.bfloat16)


def solution(mesh):
    grid = Mesh(mesh.devices.reshape(8, 4, 2, 4), ("z", "x", "c", "head"))
    blk = ("z", "x", "c")
    return jax.shard_map(
        body,
        mesh=grid,
        in_specs=(
            P(blk, "head", None),
            P(blk, "head", None),
            P(blk, "head", None),
            P(blk, "head", None),
            P(blk, "head", None),
            P(blk),
            P(),
            P(),
            P("head", blk),
        ),
        out_specs=P("head", blk),
        check_vma=False,
    )
```

```python
import functools

import jax
import jax.numpy as jnp
from jax import lax
from jax.experimental import pallas as pl
from jax.experimental.pallas import tpu as pltpu
from jax.sharding import Mesh, PartitionSpec as P

NEG = -1e30
LOG2E = 1.4426950408889634


def split3(x):
    hi = x.astype(jnp.bfloat16).astype(jnp.float32)
    rest = x - hi
    mid = rest.astype(jnp.bfloat16).astype(jnp.float32)
    low = (rest - mid).astype(jnp.bfloat16).astype(jnp.float32)
    return hi, mid, low


def seq_of(token, lens_ref, nseq):
    end = jnp.int32(0)
    which = jnp.zeros(token.shape, jnp.int32)
    for i in range(nseq):
        end = end + lens_ref[i]
        which = which + (token >= end).astype(jnp.int32)
    return which


def prepare_kernel(nseq, bounds_ref, lens_ref, k_ref, v_ref, sk_ref, sv_ref, kx_ref, vx_ref, feat_ref):
    kv, cache_dev, dh = k_ref.shape
    total = vx_ref.shape[1]
    tok_dev = sk_ref.shape[0]
    z, x, c = lax.axis_index("z"), lax.axis_index("x"), lax.axis_index("c")
    me = (z * lax.axis_size("x") + x) * 2 + c
    pos = lax.broadcasted_iota(jnp.int32, (dh, cache_dev), 1)
    row = lax.broadcasted_iota(jnp.int32, (dh, 1), 0)
    thr = jnp.full((dh, 1), total, jnp.int32)
    for i in range(nseq):
        thr = jnp.where(row == i, bounds_ref[i], thr)
    bias = jnp.where(pos >= thr, NEG, 0.0).astype(jnp.bfloat16)
    tail_pos = lax.broadcasted_iota(jnp.int32, (dh, dh), 1)
    tail_row = lax.broadcasted_iota(jnp.int32, (dh, dh), 0)
    tail = jnp.where((tail_pos >= tok_dev) & (tail_row < nseq), NEG, 0.0)
    tail = jnp.where((tail_pos < tok_dev) & (tail_row == nseq + tail_pos), 1.0, tail).astype(jnp.bfloat16)
    pad = jnp.zeros((dh - tok_dev, dh), jnp.float32)
    sk = sk_ref[...].astype(jnp.float32)
    sv = sv_ref[...].astype(jnp.float32)
    for h in range(kv):
        kx_ref[h, :dh, :cache_dev] = k_ref[h].T
        kx_ref[h, :dh, cache_dev:] = jnp.concatenate([sk[:, h], pad], axis=0).T.astype(jnp.bfloat16)
        kx_ref[h, dh:, :cache_dev] = bias
        kx_ref[h, dh:, cache_dev:] = tail
        vx_ref[h, :cache_dev, :dh] = v_ref[h]
        vx_ref[h, cache_dev:, :dh] = jnp.concatenate([sv[:, h], pad], axis=0).astype(jnp.bfloat16)
        vx_ref[h, :, dh:] = jnp.ones((total, dh), jnp.bfloat16)
    sides, ways, tile, _ = feat_ref.shape
    toks = tile // GROUP
    r = lax.broadcasted_iota(jnp.int32, (toks, dh), 0)
    lane = lax.broadcasted_iota(jnp.int32, (toks, dh), 1)
    for side in range(sides):
        core = c if side == 0 else 1 - c
        for d in range(ways):
            place = r // tok_dev * ways + (x ^ d)
            token = (place * 2 + core) * tok_dev + r % tok_dev
            seq = seq_of(token, lens_ref, nseq)
            feat = (lane == seq).astype(jnp.float32)
            for i in range(tok_dev):
                u = me * tok_dev + i
                useq = jnp.int32(0)
                end = jnp.int32(0)
                for n in range(nseq):
                    end = end + lens_ref[n]
                    useq = useq + (u >= end).astype(jnp.int32)
                seen = (seq == useq) & (u <= token)
                feat = jnp.where((lane == nseq + i) & jnp.logical_not(seen), NEG, feat)
            feat = jnp.broadcast_to(feat[:, None, :], (toks, GROUP, dh)).reshape(tile, dh)
            feat_ref[side, d] = feat.astype(jnp.bfloat16)


GROUP = 16
VMEM = pl.BlockSpec(memory_space=pltpu.VMEM)
SMEM = pl.BlockSpec(memory_space=pltpu.SMEM)


def prepare(bounds, lens, k, v, sk, sv, ways, tile):
    kv, cache_dev, dh = k.shape
    total = cache_dev + dh
    keys = jax.ShapeDtypeStruct((kv, 2 * dh, total), jnp.bfloat16)
    values = jax.ShapeDtypeStruct((kv, total, 2 * dh), jnp.bfloat16)
    return pl.pallas_call(
        functools.partial(prepare_kernel, bounds.shape[0]),
        in_specs=[SMEM] * 2 + [VMEM] * 4,
        out_specs=[VMEM] * 3,
        out_shape=[keys, values, jax.ShapeDtypeStruct((2, ways, tile, dh), jnp.bfloat16)],
        compiler_params=pltpu.CompilerParams(vmem_limit_bytes=16 * 2**20),
        cost_estimate=pl.CostEstimate(flops=2 * kv * total * dh * 8, bytes_accessed=8 * 2**20, transcendentals=0),
    )(bounds, lens, k, v, sk, sv)


def stat_block(lines, dh):
    sub = lax.broadcasted_iota(jnp.int32, (8, dh), 0)
    stat = jnp.zeros((8, dh), jnp.float32)
    for h, line in enumerate(lines):
        for i, part in enumerate(split3(line)):
            stat = jnp.where(sub == 3 * h + i, part, stat)
    return stat.astype(jnp.bfloat16)


def line_of(block, h):
    block = block.astype(jnp.float32)
    return block[3 * h : 3 * h + 1] + block[3 * h + 1 : 3 * h + 2] + block[3 * h + 2 : 3 * h + 3]


def rows_of(ref, at, g, h, tok_dev, heads, group, dh):
    per = dh // (tok_dev * group)
    where = pl.ds(g * per, per)
    parts = [ref[(*at, where, pl.ds(t * heads + h * group, group), slice(None))] for t in range(tok_dev)]
    return jnp.stack(parts, axis=1).reshape(dh, dh).astype(jnp.float32)


def attend_kernel(jobs, n_q, plain, merging, *refs):
    q_refs = refs[:n_q]
    feat_ref, kx_ref, vx_ref = refs[n_q : n_q + 3]
    rest = refs[n_q + 3 :]
    if merging:
        own_refs, (got_ref, out_ref) = rest[:plain], rest[plain : plain + 2]
        outs, rest = [out_ref], rest[plain + 2 :]
    else:
        n_out = 1 + max(part[3] for job in jobs for part in job)
        outs, rest = list(rest[:n_out]), rest[n_out:]
    sa_ref, sb_ref = rest
    count, tok_dev, heads, dh = q_refs[0].shape
    kv, _, total = kx_ref.shape
    group = heads // kv
    n = count * tok_dev * group
    per = dh // (tok_dev * group)
    groups = n // dh
    scale = LOG2E * dh ** (-0.5)
    edges = [0, 512, 1024, 1536, total]
    spans = list(zip(edges[:-1], edges[1:]))
    diag = lax.broadcasted_iota(jnp.int32, (dh, dh), 0) == lax.broadcasted_iota(jnp.int32, (dh, dh), 1)
    x = lax.axis_index("x")

    def load(job, h):
        q = [q_refs[part[0]][:, :, h * group : (h + 1) * group, :].reshape(n, dh) for part in job]
        feat = [feat_ref[part[1], part[2]] for part in job]
        rows = [jnp.concatenate(pair, axis=1) for pair in zip(q, feat)]
        return rows[0] if len(rows) == 1 else jnp.concatenate(rows, axis=0)

    def score(qx, h, s_ref, span, top):
        s = jnp.dot(qx, kx_ref[h, :, span[0] : span[1]], preferred_element_type=jnp.float32)
        s_ref[:, span[0] : span[1]] = s
        for i in range((span[1] - span[0]) // dh):
            part = s[:, i * dh : (i + 1) * dh]
            top = part if top is None else jnp.maximum(top, part)
        return top

    def merge_weights(mine, theirs):
        high = jnp.maximum(mine, theirs)
        a, b = jnp.exp2(mine - high), jnp.exp2(theirs - high)
        both = a + b
        return a / both, b / both, high + jnp.log2(both)

    def column(line):
        return jnp.sum(jnp.where(diag, line, 0.0), axis=1, keepdims=True)

    def line(column):
        return jnp.sum(jnp.where(diag, column, 0.0), axis=0, keepdims=True)

    def put(job, g, h, value):
        value = value.reshape(per, tok_dev, group, dh).astype(jnp.bfloat16)
        for t in range(tok_dev):
            place = pl.ds(t * heads + h * group, group)
            if merging:
                pairs = pl.ds((t * heads + h * group) // 2, group // 2)
                outs[0][pl.ds(g * per, per), x ^ job[2], pairs, :, :] = value[:, t].reshape(per, group // 2, 2, dh)
            else:
                outs[job[3]][(*job[4], pl.ds(g * per, per), place, slice(None))] = value[:, t]

    def put_stat(job, g, lines):
        stat = stat_block(lines, dh)
        if merging:
            wide = stat.astype(jnp.float32)
            turned = [wide] + [pltpu.roll(wide, k * (dh // per), 1) for k in range(1, per)]
            quarter = lax.broadcasted_iota(jnp.int32, (1, dh), 1) // (dh // per)
            for i in range(per):
                pair = []
                for base in (0, per):
                    row = jnp.zeros((1, dh), jnp.float32)
                    for k in range(per):
                        if base + k < 6:
                            row = jnp.where(quarter == k, turned[(k - i) % per][base + k : base + k + 1], row)
                    pair.append(row)
                pair = jnp.concatenate(pair, axis=0).astype(jnp.bfloat16)
                outs[0][g * per + i, x ^ job[2], tok_dev * heads // 2, :, :] = pair
            return
        for i in range(per):
            outs[job[3]][(*job[4], g * per + i, slice(tok_dev * heads, None), slice(None))] = stat

    def half(job, h, s_ref, lanes_top, later):
        top = jnp.max(lanes_top, axis=1, keepdims=True)
        acc = None
        next_top = None
        if later is not None:
            next_qx, next_h, next_ref = load(*later[:2]), later[1], later[2]
        for span in spans:
            if later is not None:
                next_top = score(next_qx, next_h, next_ref, span, next_top)
            p = jnp.exp2((s_ref[:, span[0] : span[1]] - top) * scale).astype(jnp.bfloat16)
            term = jnp.dot(p, vx_ref[h, span[0] : span[1], :], preferred_element_type=jnp.float32)
            acc = term if acc is None else acc + term
        total_l = acc[:, dh:]
        lines = []
        for at in range(groups * len(job)):
            part, g = job[at // groups], at % groups
            rows = slice(at * dh, (at + 1) * dh)
            top_line, total_line = line(top[rows]), line(total_l[rows])
            mine = jnp.where(top_line > 0.5 * NEG, top_line * scale + jnp.log2(total_line), NEG)
            if merging:
                theirs = line_of(got_ref[part[2], g * per, tok_dev * heads :, :], h)
                o_theirs = rows_of(got_ref, (part[2],), g, h, tok_dev, heads, group, dh)
                a, b, mine = merge_weights(mine, theirs)
                value = acc[rows, :dh] * column(a / total_line) + o_theirs * column(b)
            else:
                value = acc[rows, :dh] / total_l[rows]
            put(part, g, h, value)
            lines.append(mine)
        return lines, next_top

    first = load(jobs[0], 0)
    top = None
    for span in spans:
        top = score(first, 0, sa_ref, span, top)
    if merging:
        for d in range(plain):
            for g in range(groups):
                lines = []
                for h in range(kv):
                    at = (g * per, slice(tok_dev * heads, None), slice(None))
                    pair = ((own_refs[d], ()), (got_ref, (d,)))
                    lse = [line_of(ref[(*first_at, *at)], h) for ref, first_at in pair]
                    o = [rows_of(ref, first_at, g, h, tok_dev, heads, group, dh) for ref, first_at in pair]
                    a, b, mine = merge_weights(*lse)
                    put((0, 0, d), g, h, o[0] * column(a) + o[1] * column(b))
                    lines.append(mine)
                put_stat((0, 0, d), g, lines)
    for i, job in enumerate(jobs):
        lines_a, top = half(job, 0, sa_ref, top, (job, 1, sb_ref))
        later = (jobs[i + 1], 0, sa_ref) if i + 1 < len(jobs) else None
        lines_b, top = half(job, 1, sb_ref, top, later)
        for at in range(groups * len(job)):
            put_stat(job[at // groups], at % groups, (lines_a[at], lines_b[at]))


def attend(jobs, queries, feat, kx, vx, out_shapes, merge_with=()):
    count, tok_dev, heads, dh = queries[0].shape
    kv, _, total = kx.shape
    n = count * tok_dev * heads // kv * max(len(job) for job in jobs)
    work = n * kv * len(jobs) * total
    shapes = [jax.ShapeDtypeStruct(shape, jnp.bfloat16) for shape in out_shapes]
    return pl.pallas_call(
        functools.partial(attend_kernel, jobs, len(queries), max(len(merge_with) - 1, 0), bool(merge_with)),
        in_specs=[VMEM] * (len(queries) + 3 + len(merge_with)),
        out_specs=[VMEM] * len(shapes),
        out_shape=shapes,
        scratch_shapes=[
            pltpu.VMEM((n, total), jnp.float32),
            pltpu.VMEM((n, total), jnp.float32),
        ],
        compiler_params=pltpu.CompilerParams(vmem_limit_bytes=26 * 2**20),
        cost_estimate=pl.CostEstimate(flops=8 * work * dh, bytes_accessed=5 * 2**20, transcendentals=work),
    )(*queries, feat, kx, vx, *merge_with)


def merge_kernel(rows, in_ref, out_ref, flat_ref):
    count, pairs, _, dh = in_ref.shape
    kv = 2
    first, second = [], []
    for i in range(count):
        block = in_ref[i, pairs - 1].astype(jnp.float32)
        first.append(block[0:1])
        second.append(block[1:2])
    first, second = jnp.concatenate(first, axis=0), jnp.concatenate(second, axis=0)
    at = lambda a, k: pltpu.roll(a, dh - k * rows, 1) if k else a
    lines = [at(first, 0) + at(first, 1) + at(first, 2), at(first, 3) + at(second, 0) + at(second, 1)]
    for h in range(kv):
        lse = lines[h]
        high = jnp.max(lse, axis=0, keepdims=True)
        w = jnp.exp2(lse - high)
        w = w / jnp.sum(w, axis=0, keepdims=True)
        w = jnp.concatenate([w, jnp.zeros((dh - count, dh), jnp.float32)], axis=0)
        wt = w.T
        mine = wt[:rows]
        group = rows // 2
        acc = jnp.zeros((rows, dh), jnp.float32)
        for i in range(count):
            blocks = [in_ref[i, pl.ds(t * group + h * (group // 2), group // 2)].reshape(group, dh) for t in range(2)]
            acc = acc + mine[:, i : i + 1] * jnp.concatenate(blocks, axis=0).astype(jnp.float32)
        for t in range(2):
            for j in range(group):
                at = (h * group + j) * dh
                flat_ref[t : t + 1, at : at + dh] = acc[t * group + j : t * group + j + 1]
    value = flat_ref[...].astype(jnp.bfloat16)
    for i in range(count):
        out_ref[i] = value


def merge(got, rows):
    count, _, _, dh = got.shape
    width = 2 * rows // 2 * dh
    return pl.pallas_call(
        functools.partial(merge_kernel, rows),
        out_shape=jax.ShapeDtypeStruct((count, 2, width), jnp.bfloat16),
        in_specs=[pl.BlockSpec(memory_space=pltpu.VMEM)],
        out_specs=pl.BlockSpec(memory_space=pltpu.VMEM),
        scratch_shapes=[pltpu.VMEM((2, width), jnp.float32)],
        compiler_params=pltpu.CompilerParams(vmem_limit_bytes=16 * 2**20),
    )(got)


def body(queries, cache_keys, cache_values, stretch_keys, stretch_values, valid_lens, offsets, seq_lengths, out_weight):
    tok_dev, heads, dh = queries.shape
    kv = cache_keys.shape[1]
    group = heads // kv
    count = lax.axis_size("z") * lax.axis_size("x")
    rows = tok_dev * group
    c = lax.axis_index("c")
    zx = ("z", "x")
    swap = lambda a: lax.ppermute(a, "c", [(0, 1), (1, 0)])
    everywhere = lambda a: lax.all_to_all(a, zx, 0, 0, tiled=True)

    deep, ways = lax.axis_size("z"), lax.axis_size("x")
    tile = deep * rows
    mine = [lax.all_to_all(jnp.broadcast_to(queries[None], (deep,) + queries.shape), "z", 0, 0, tiled=True)]
    values = cache_values.transpose(1, 0, 2)
    me = (lax.axis_index("z") * ways + lax.axis_index("x")) * 2 + c
    bounds = jnp.minimum(valid_lens, offsets - me * cache_keys.shape[0])
    mine[0], cache_keys, values, bounds = lax.optimization_barrier((mine[0], cache_keys, values, bounds))
    keys = cache_keys.transpose(1, 0, 2)
    kx, vx, feat = prepare(bounds, seq_lengths, keys, values, stretch_keys, stretch_values, ways, tile)
    for d in range(1, ways):
        mine.append(lax.ppermute(mine[0], "x", [(i, i ^ d) for i in range(ways)]))
    block = (deep, tok_dev * heads + 8, dh)
    near = [attend([((0, 0, d, 0, ()),)], [mine[d]], feat, kx, vx, [block])[0] for d in range(3)]
    *late, near[0] = lax.optimization_barrier((*mine, near[0]))
    theirs = [swap(q) for q in late]
    *theirs, near[1] = lax.optimization_barrier((*theirs, near[1]))
    jobs = [tuple((d, 1, d, 0, (d,)) for d in pair) for pair in ((0, 1), (2, 3))]
    (away,) = attend(jobs, theirs, feat, kx, vx, [(ways,) + block])
    rest = range(len(near), ways)
    jobs = [((i, 0, d, 0, ()),) for i, d in enumerate(rest)]
    merge_with = (*near, swap(away))
    (part,) = attend(jobs, [mine[d] for d in rest], feat, kx, vx, [(deep, ways, tok_dev * heads // 2 + 1, 2, dh)], merge_with)
    part = part.reshape((count,) + part.shape[2:])
    attended = everywhere(merge(everywhere(part), rows))
    attended_other = swap(attended)
    width = attended.shape[-1]
    project = lambda a: jnp.dot(a.reshape(count * tok_dev, width), out_weight, preferred_element_type=jnp.float32)
    near, far = project(attended), project(attended_other)
    ways = lax.axis_size("head")
    cols = out_weight.shape[1]
    terms = jnp.stack([a.reshape(ways, count // ways, tok_dev, cols) for a in (near, far)], axis=1)
    y = lax.axis_index("head")
    piece = lambda d: lax.dynamic_index_in_dim(terms, y ^ d, 0, keepdims=False)
    total = piece(0)
    for d in range(1, ways):
        total = total + lax.ppermute(piece(d), "head", [(i, i ^ d) for i in range(ways)])
    terms = total
    first = jnp.where(c == 0, terms[0], terms[1])
    second = jnp.where(c == 0, terms[1], terms[0])
    return jnp.stack([first, second], axis=1).reshape(-1, cols).astype(jnp.bfloat16)


def solution(mesh):
    grid = Mesh(mesh.devices.reshape(8, 4, 2, 4), ("z", "x", "c", "head"))
    blk = ("z", "x", "c")
    return jax.shard_map(
        body,
        mesh=grid,
        in_specs=(
            P(blk, "head", None),
            P(blk, "head", None),
            P(blk, "head", None),
            P(blk, "head", None),
            P(blk, "head", None),
            P(blk),
            P(),
            P(),
            P("head", blk),
        ),
        out_specs=P("head", blk),
        check_vma=False,
    )
```

```python
import functools

import jax
import jax.numpy as jnp
from jax import lax
from jax.experimental import pallas as pl
from jax.experimental.pallas import tpu as pltpu
from jax.sharding import Mesh, PartitionSpec as P

NEG = -1e30
LOG2E = 1.4426950408889634


def split3(x):
    hi = x.astype(jnp.bfloat16).astype(jnp.float32)
    rest = x - hi
    mid = rest.astype(jnp.bfloat16).astype(jnp.float32)
    low = (rest - mid).astype(jnp.bfloat16).astype(jnp.float32)
    return hi, mid, low


def seq_of(token, lens_ref, nseq):
    end = jnp.int32(0)
    which = jnp.zeros(token.shape, jnp.int32)
    for i in range(nseq):
        end = end + lens_ref[i]
        which = which + (token >= end).astype(jnp.int32)
    return which


def prepare_kernel(nseq, bounds_ref, lens_ref, k_ref, v_ref, sk_ref, sv_ref, kx_ref, vx_ref, feat_ref):
    kv, cache_dev, dh = k_ref.shape
    total = vx_ref.shape[1]
    tok_dev = sk_ref.shape[0]
    z, x, c = lax.axis_index("z"), lax.axis_index("x"), lax.axis_index("c")
    me = (z * lax.axis_size("x") + x) * 2 + c
    pos = lax.broadcasted_iota(jnp.int32, (dh, cache_dev), 1)
    row = lax.broadcasted_iota(jnp.int32, (dh, 1), 0)
    thr = jnp.full((dh, 1), total, jnp.int32)
    for i in range(nseq):
        thr = jnp.where(row == i, bounds_ref[i], thr)
    bias = jnp.where(pos >= thr, NEG, 0.0).astype(jnp.bfloat16)
    tail_pos = lax.broadcasted_iota(jnp.int32, (dh, dh), 1)
    tail_row = lax.broadcasted_iota(jnp.int32, (dh, dh), 0)
    tail = jnp.where((tail_pos >= tok_dev) & (tail_row < nseq), NEG, 0.0)
    tail = jnp.where((tail_pos < tok_dev) & (tail_row == nseq + tail_pos), 1.0, tail).astype(jnp.bfloat16)
    pad = jnp.zeros((dh - tok_dev, dh), jnp.float32)
    sk = sk_ref[...].astype(jnp.float32)
    sv = sv_ref[...].astype(jnp.float32)
    for h in range(kv):
        kx_ref[h, :dh, :cache_dev] = k_ref[h].T
        kx_ref[h, :dh, cache_dev:] = jnp.concatenate([sk[:, h], pad], axis=0).T.astype(jnp.bfloat16)
        kx_ref[h, dh:, :cache_dev] = bias
        kx_ref[h, dh:, cache_dev:] = tail
        vx_ref[h, :cache_dev, :dh] = v_ref[h]
        vx_ref[h, cache_dev:, :dh] = jnp.concatenate([sv[:, h], pad], axis=0).astype(jnp.bfloat16)
        vx_ref[h, :, dh:] = jnp.ones((total, dh), jnp.bfloat16)
    sides, ways, tile, _ = feat_ref.shape
    toks = tile // GROUP
    r = lax.broadcasted_iota(jnp.int32, (toks, dh), 0)
    lane = lax.broadcasted_iota(jnp.int32, (toks, dh), 1)
    for side in range(sides):
        core = c if side == 0 else 1 - c
        for d in range(ways):
            place = r // tok_dev * ways + (x ^ d)
            token = (place * 2 + core) * tok_dev + r % tok_dev
            seq = seq_of(token, lens_ref, nseq)
            feat = (lane == seq).astype(jnp.float32)
            for i in range(tok_dev):
                u = me * tok_dev + i
                useq = jnp.int32(0)
                end = jnp.int32(0)
                for n in range(nseq):
                    end = end + lens_ref[n]
                    useq = useq + (u >= end).astype(jnp.int32)
                seen = (seq == useq) & (u <= token)
                feat = jnp.where((lane == nseq + i) & jnp.logical_not(seen), NEG, feat)
            feat = jnp.broadcast_to(feat[:, None, :], (toks, GROUP, dh)).reshape(tile, dh)
            feat_ref[side, d] = feat.astype(jnp.bfloat16)


GROUP = 16
VMEM = pl.BlockSpec(memory_space=pltpu.VMEM)
SMEM = pl.BlockSpec(memory_space=pltpu.SMEM)


def prepare(bounds, lens, k, v, sk, sv, ways, tile):
    kv, cache_dev, dh = k.shape
    total = cache_dev + dh
    keys = jax.ShapeDtypeStruct((kv, 2 * dh, total), jnp.bfloat16)
    values = jax.ShapeDtypeStruct((kv, total, 2 * dh), jnp.bfloat16)
    return pl.pallas_call(
        functools.partial(prepare_kernel, bounds.shape[0]),
        in_specs=[SMEM] * 2 + [VMEM] * 4,
        out_specs=[VMEM] * 3,
        out_shape=[keys, values, jax.ShapeDtypeStruct((2, ways, tile, dh), jnp.bfloat16)],
        compiler_params=pltpu.CompilerParams(vmem_limit_bytes=16 * 2**20),
        cost_estimate=pl.CostEstimate(flops=2 * kv * total * dh * 8, bytes_accessed=8 * 2**20, transcendentals=0),
    )(bounds, lens, k, v, sk, sv)


def stat_block(lines, dh):
    sub = lax.broadcasted_iota(jnp.int32, (8, dh), 0)
    stat = jnp.zeros((8, dh), jnp.float32)
    for h, line in enumerate(lines):
        for i, part in enumerate(split3(line)):
            stat = jnp.where(sub == 3 * h + i, part, stat)
    return stat.astype(jnp.bfloat16)


def line_of(block, h):
    block = block.astype(jnp.float32)
    return block[3 * h : 3 * h + 1] + block[3 * h + 1 : 3 * h + 2] + block[3 * h + 2 : 3 * h + 3]


def rows_of(ref, at, g, h, tok_dev, heads, group, dh):
    per = dh // (tok_dev * group)
    where = pl.ds(g * per, per)
    parts = [ref[(*at, where, pl.ds(t * heads + h * group, group), slice(None))] for t in range(tok_dev)]
    return jnp.stack(parts, axis=1).reshape(dh, dh).astype(jnp.float32)


def attend_kernel(jobs, n_q, plain, merging, *refs):
    q_refs = refs[:n_q]
    feat_ref, kx_ref, vx_ref = refs[n_q : n_q + 3]
    rest = refs[n_q + 3 :]
    if merging:
        own_refs, (got_ref, out_ref) = rest[:plain], rest[plain : plain + 2]
        outs, rest = [out_ref], rest[plain + 2 :]
    else:
        n_out = 1 + max(part[3] for job in jobs for part in job)
        outs, rest = list(rest[:n_out]), rest[n_out:]
    sa_ref, sb_ref = rest
    count, tok_dev, heads, dh = q_refs[0].shape
    kv, _, total = kx_ref.shape
    group = heads // kv
    n = count * tok_dev * group
    per = dh // (tok_dev * group)
    groups = n // dh
    scale = LOG2E * dh ** (-0.5)
    edges = [0, 512, 1024, 1536, total]
    spans = list(zip(edges[:-1], edges[1:]))
    diag = lax.broadcasted_iota(jnp.int32, (dh, dh), 0) == lax.broadcasted_iota(jnp.int32, (dh, dh), 1)
    x = lax.axis_index("x")

    def load(job, h):
        q = [q_refs[part[0]][:, :, h * group : (h + 1) * group, :].reshape(n, dh) for part in job]
        feat = [feat_ref[part[1], part[2]] for part in job]
        rows = [jnp.concatenate(pair, axis=1) for pair in zip(q, feat)]
        return rows[0] if len(rows) == 1 else jnp.concatenate(rows, axis=0)

    def score(qx, h, s_ref, span, top):
        s = jnp.dot(qx, kx_ref[h, :, span[0] : span[1]], preferred_element_type=jnp.float32)
        s_ref[:, span[0] : span[1]] = s
        for i in range((span[1] - span[0]) // dh):
            part = s[:, i * dh : (i + 1) * dh]
            top = part if top is None else jnp.maximum(top, part)
        return top

    def merge_weights(mine, theirs):
        high = jnp.maximum(mine, theirs)
        a, b = jnp.exp2(mine - high), jnp.exp2(theirs - high)
        both = a + b
        return a / both, b / both, high + jnp.log2(both)

    def column(line):
        return jnp.sum(jnp.where(diag, line, 0.0), axis=1, keepdims=True)

    def line(column):
        return jnp.sum(jnp.where(diag, column, 0.0), axis=0, keepdims=True)

    def put(job, g, h, value):
        value = value.reshape(per, tok_dev, group, dh).astype(jnp.bfloat16)
        for t in range(tok_dev):
            place = pl.ds(t * heads + h * group, group)
            if merging:
                pairs = pl.ds((t * heads + h * group) // 2, group // 2)
                outs[0][pl.ds(g * per, per), x ^ job[2], pairs, :, :] = value[:, t].reshape(per, group // 2, 2, dh)
            else:
                outs[job[3]][(*job[4], pl.ds(g * per, per), place, slice(None))] = value[:, t]

    def put_stat(job, g, lines):
        stat = stat_block(lines, dh)
        if merging:
            wide = stat.astype(jnp.float32)
            turned = [wide] + [pltpu.roll(wide, k * (dh // per), 1) for k in range(1, per)]
            quarter = lax.broadcasted_iota(jnp.int32, (1, dh), 1) // (dh // per)
            for i in range(per):
                pair = []
                for base in (0, per):
                    row = jnp.zeros((1, dh), jnp.float32)
                    for k in range(per):
                        if base + k < 6:
                            row = jnp.where(quarter == k, turned[(k - i) % per][base + k : base + k + 1], row)
                    pair.append(row)
                pair = jnp.concatenate(pair, axis=0).astype(jnp.bfloat16)
                outs[0][g * per + i, x ^ job[2], tok_dev * heads // 2, :, :] = pair
            return
        for i in range(per):
            outs[job[3]][(*job[4], g * per + i, slice(tok_dev * heads, None), slice(None))] = stat

    def half(job, h, s_ref, lanes_top, later):
        top = jnp.max(lanes_top, axis=1, keepdims=True)
        acc = None
        next_top = None
        if later is not None:
            next_qx, next_h, next_ref = load(*later[:2]), later[1], later[2]
        for span in spans:
            if later is not None:
                next_top = score(next_qx, next_h, next_ref, span, next_top)
            p = jnp.exp2((s_ref[:, span[0] : span[1]] - top) * scale).astype(jnp.bfloat16)
            term = jnp.dot(p, vx_ref[h, span[0] : span[1], :], preferred_element_type=jnp.float32)
            acc = term if acc is None else acc + term
        total_l = acc[:, dh:]
        lines = []
        for at in range(groups * len(job)):
            part, g = job[at // groups], at % groups
            rows = slice(at * dh, (at + 1) * dh)
            top_line, total_line = line(top[rows]), line(total_l[rows])
            mine = jnp.where(top_line > 0.5 * NEG, top_line * scale + jnp.log2(total_line), NEG)
            if merging:
                theirs = line_of(got_ref[part[2], g * per, tok_dev * heads :, :], h)
                o_theirs = rows_of(got_ref, (part[2],), g, h, tok_dev, heads, group, dh)
                a, b, mine = merge_weights(mine, theirs)
                value = acc[rows, :dh] * column(a / total_line) + o_theirs * column(b)
            else:
                value = acc[rows, :dh] / total_l[rows]
            put(part, g, h, value)
            lines.append(mine)
        return lines, next_top

    first = load(jobs[0], 0)
    top = None
    for span in spans:
        top = score(first, 0, sa_ref, span, top)
    if merging:
        for d in range(plain):
            for g in range(groups):
                lines = []
                for h in range(kv):
                    at = (g * per, slice(tok_dev * heads, None), slice(None))
                    pair = ((own_refs[d], ()), (got_ref, (d,)))
                    lse = [line_of(ref[(*first_at, *at)], h) for ref, first_at in pair]
                    o = [rows_of(ref, first_at, g, h, tok_dev, heads, group, dh) for ref, first_at in pair]
                    a, b, mine = merge_weights(*lse)
                    put((0, 0, d), g, h, o[0] * column(a) + o[1] * column(b))
                    lines.append(mine)
                put_stat((0, 0, d), g, lines)
    for i, job in enumerate(jobs):
        lines_a, top = half(job, 0, sa_ref, top, (job, 1, sb_ref))
        later = (jobs[i + 1], 0, sa_ref) if i + 1 < len(jobs) else None
        lines_b, top = half(job, 1, sb_ref, top, later)
        for at in range(groups * len(job)):
            put_stat(job[at // groups], at % groups, (lines_a[at], lines_b[at]))


def attend(jobs, queries, feat, kx, vx, out_shapes, merge_with=()):
    count, tok_dev, heads, dh = queries[0].shape
    kv, _, total = kx.shape
    n = count * tok_dev * heads // kv * max(len(job) for job in jobs)
    work = n * kv * len(jobs) * total
    shapes = [jax.ShapeDtypeStruct(shape, jnp.bfloat16) for shape in out_shapes]
    return pl.pallas_call(
        functools.partial(attend_kernel, jobs, len(queries), max(len(merge_with) - 1, 0), bool(merge_with)),
        in_specs=[VMEM] * (len(queries) + 3 + len(merge_with)),
        out_specs=[VMEM] * len(shapes),
        out_shape=shapes,
        scratch_shapes=[
            pltpu.VMEM((n, total), jnp.float32),
            pltpu.VMEM((n, total), jnp.float32),
        ],
        compiler_params=pltpu.CompilerParams(vmem_limit_bytes=26 * 2**20),
        cost_estimate=pl.CostEstimate(flops=8 * work * dh, bytes_accessed=5 * 2**20, transcendentals=work),
    )(*queries, feat, kx, vx, *merge_with)


def merge_kernel(rows, in_ref, out_ref, flat_ref):
    count, pairs, _, dh = in_ref.shape
    kv = 2
    first, second = [], []
    for i in range(count):
        block = in_ref[i, pairs - 1].astype(jnp.float32)
        first.append(block[0:1])
        second.append(block[1:2])
    first, second = jnp.concatenate(first, axis=0), jnp.concatenate(second, axis=0)
    at = lambda a, k: pltpu.roll(a, dh - k * rows, 1) if k else a
    lines = [at(first, 0) + at(first, 1) + at(first, 2), at(first, 3) + at(second, 0) + at(second, 1)]
    for h in range(kv):
        lse = lines[h]
        high = jnp.max(lse, axis=0, keepdims=True)
        w = jnp.exp2(lse - high)
        w = w / jnp.sum(w, axis=0, keepdims=True)
        w = jnp.concatenate([w, jnp.zeros((dh - count, dh), jnp.float32)], axis=0)
        wt = w.T
        mine = wt[:rows]
        group = rows // 2
        acc = jnp.zeros((rows, dh), jnp.float32)
        for i in range(count):
            blocks = [in_ref[i, pl.ds(t * group + h * (group // 2), group // 2)].reshape(group, dh) for t in range(2)]
            acc = acc + mine[:, i : i + 1] * jnp.concatenate(blocks, axis=0).astype(jnp.float32)
        for t in range(2):
            for j in range(group):
                at = (h * group + j) * dh
                flat_ref[t : t + 1, at : at + dh] = acc[t * group + j : t * group + j + 1]
    value = flat_ref[...].astype(jnp.bfloat16)
    for i in range(count):
        out_ref[i] = value


def merge(got, rows):
    count, _, _, dh = got.shape
    width = 2 * rows // 2 * dh
    return pl.pallas_call(
        functools.partial(merge_kernel, rows),
        out_shape=jax.ShapeDtypeStruct((count, 2, width), jnp.bfloat16),
        in_specs=[pl.BlockSpec(memory_space=pltpu.VMEM)],
        out_specs=pl.BlockSpec(memory_space=pltpu.VMEM),
        scratch_shapes=[pltpu.VMEM((2, width), jnp.float32)],
        compiler_params=pltpu.CompilerParams(vmem_limit_bytes=16 * 2**20),
    )(got)


def body(queries, cache_keys, cache_values, stretch_keys, stretch_values, valid_lens, offsets, seq_lengths, out_weight):
    tok_dev, heads, dh = queries.shape
    kv = cache_keys.shape[1]
    group = heads // kv
    count = lax.axis_size("z") * lax.axis_size("x")
    rows = tok_dev * group
    c = lax.axis_index("c")
    zx = ("z", "x")
    swap = lambda a: lax.ppermute(a, "c", [(0, 1), (1, 0)])
    everywhere = lambda a: lax.all_to_all(a, zx, 0, 0, tiled=True)

    deep, ways = lax.axis_size("z"), lax.axis_size("x")
    tile = deep * rows
    mine = [lax.all_to_all(jnp.broadcast_to(queries[None], (deep,) + queries.shape), "z", 0, 0, tiled=True)]
    values = cache_values.transpose(1, 0, 2)
    me = (lax.axis_index("z") * ways + lax.axis_index("x")) * 2 + c
    bounds = jnp.minimum(valid_lens, offsets - me * cache_keys.shape[0])
    mine[0], cache_keys, values, bounds = lax.optimization_barrier((mine[0], cache_keys, values, bounds))
    keys = cache_keys.transpose(1, 0, 2)
    kx, vx, feat = prepare(bounds, seq_lengths, keys, values, stretch_keys, stretch_values, ways, tile)
    for d in range(1, ways):
        mine.append(lax.ppermute(mine[0], "x", [(i, i ^ d) for i in range(ways)]))
    block = (deep, tok_dev * heads + 8, dh)
    near = [attend([((0, 0, d, 0, ()),)], [mine[d]], feat, kx, vx, [block])[0] for d in range(3)]
    *late, near[0] = lax.optimization_barrier((*mine, near[0]))
    theirs = [swap(q) for q in late]
    *theirs, near[1] = lax.optimization_barrier((*theirs, near[1]))
    jobs = [tuple((d, 1, d, 0, (d,)) for d in pair) for pair in ((0, 1), (2, 3))]
    (away,) = attend(jobs, theirs, feat, kx, vx, [(ways,) + block])
    rest = range(len(near), ways)
    jobs = [((i, 0, d, 0, ()),) for i, d in enumerate(rest)]
    merge_with = (*near, swap(away))
    (part,) = attend(jobs, [mine[d] for d in rest], feat, kx, vx, [(deep, ways, tok_dev * heads // 2 + 1, 2, dh)], merge_with)
    part = part.reshape((count,) + part.shape[2:])
    attended = everywhere(merge(everywhere(part), rows))
    attended_other = swap(attended)
    width = attended.shape[-1]
    project = lambda a: jnp.dot(a.reshape(count * tok_dev, width), out_weight, preferred_element_type=jnp.float32)
    near, far = project(attended), project(attended_other)
    ways = lax.axis_size("head")
    cols = out_weight.shape[1]
    terms = jnp.stack([a.reshape(ways, count // ways, tok_dev, cols) for a in (near, far)], axis=1)
    y = lax.axis_index("head")
    piece = lambda d: lax.dynamic_index_in_dim(terms, y ^ d, 0, keepdims=False)
    total = piece(0)
    for d in range(1, ways):
        total = total + lax.ppermute(piece(d).astype(jnp.bfloat16), "head", [(i, i ^ d) for i in range(ways)]).astype(jnp.float32)
    terms = total
    first = jnp.where(c == 0, terms[0], terms[1])
    second = jnp.where(c == 0, terms[1], terms[0])
    return jnp.stack([first, second], axis=1).reshape(-1, cols).astype(jnp.bfloat16)


def solution(mesh):
    grid = Mesh(mesh.devices.reshape(8, 4, 2, 4), ("z", "x", "c", "head"))
    blk = ("z", "x", "c")
    return jax.shard_map(
        body,
        mesh=grid,
        in_specs=(
            P(blk, "head", None),
            P(blk, "head", None),
            P(blk, "head", None),
            P(blk, "head", None),
            P(blk, "head", None),
            P(blk),
            P(),
            P(),
            P("head", blk),
        ),
        out_specs=P("head", blk),
        check_vma=False,
    )
```
